256 devices in a mesh: seq: 64 (over z_lo, x, y), head: 4 (over z_hi, core).
Axes of the slice: x: 4, y: 4, z: 8 (z_hi: 2, z_lo: 4; z = z_hi * 4 + z_lo), core: 2. Of those that a mesh axis runs over, the one named last changes fastest.
Arguments:
- tile_query: bfloat16 [768, 32768], P('head', 'seq')
- tile_key: bfloat16 [768, 32768], P('head', 'seq')
- tile_value: bfloat16 [768, 32768], P('head', 'seq'), may hold values from -6 to 6
- out_cotangent: bfloat16 [768, 32768], P('head', 'seq'), may hold values from -6 to 6
Outputs:
- attended: bfloat16 [768, 32768], P('head', 'seq')
- grad_query: bfloat16 [768, 32768], P('head', 'seq')
- grad_key: bfloat16 [768, 32768], P('head', 'seq')
- grad_value: bfloat16 [768, 32768], P('head', 'seq')
The draws below stay inside these ranges and needn't reach their ends.
All inputs are finite; a program needn't handle non-finite values.
Results may differ from the reference program's by a relative error of at most 0.023.
Values may be sent and summed in bfloat16 or wider, within the bound.
A program may use at most 192 MiB of HBM per device.

```python
import jax
import jax.numpy as jnp
from jax import lax

H = 12
E = 64
TOK_DEV = 512
TOKENS = 32768
LEVELS = 7


def draw_tile_query(key, part):
    key = jax.random.fold_in(key, 11)
    base = jnp.clip(jax.random.normal(key, (TOKENS, H * E), jnp.float32), -4.5, 4.5)
    return base.T.astype(jnp.bfloat16)


def draw_tile_key(key, part):
    key = jax.random.fold_in(key, 23)
    base = jnp.clip(jax.random.normal(key, (TOKENS, H * E), jnp.float32), -4.5, 4.5)
    return base.T.astype(jnp.bfloat16)


def block_scale(key, shape, split, smallest, high):
    level, own = 1.0, jax.random.fold_in(key, 6)
    for axis_at, parts in split:
        steps = jnp.exp(jax.random.uniform(jax.random.fold_in(own, axis_at), (parts,), jnp.float32, smallest / len(split), high / len(split)))
        level = level * jnp.repeat(steps, shape[axis_at] // parts).reshape([-1 if axis == axis_at else 1 for axis in range(len(shape))])
    return level


def bell_draw(key, shape, scale, limit, pieces=(), kind=jnp.bfloat16):
    level = block_scale(key, shape, pieces, -0.22, 0.18) if pieces else 1.0
    values = jax.random.normal(key, shape, jnp.float32) * scale * level
    return jnp.minimum(jnp.maximum(values, -limit), limit).astype(kind)


def setup_inputs(seed: int = 0) -> dict:
    keys = jax.random.split(jax.random.key(seed), 5)
    tile_query = draw_tile_query(jax.random.fold_in(keys[4], 71), 0)
    tile_key = draw_tile_key(jax.random.fold_in(keys[4], 71), 0)
    tile_value = bell_draw(keys[2], (H * E, TOKENS), 1.0, 6.0, ((0, 4), (1, 64)))
    out_cotangent = bell_draw(keys[3], (H * E, TOKENS), 1.0, 6.0, ((0, 4), (1, 64)))
    return dict(tile_query=tile_query, tile_key=tile_key, tile_value=tile_value, out_cotangent=out_cotangent)


NEG_FILL = -1e30


def rounded(values):
    return lax.optimization_barrier(values.astype(jnp.bfloat16)).astype(jnp.float32)


def reference(tile_query, tile_key, tile_value, out_cotangent):
    tile_query = tile_query.T
    tile_key = tile_key.T
    tile_value = tile_value.T
    out_cotangent = out_cotangent.T
    score_scale = E ** -0.5
    out_cols = []
    gq_cols = []
    gk_cols = []
    gv_cols = []
    for head_index in range(H):
        first_col = head_index * E
        query_head = tile_query[:, first_col:first_col + E]
        key_head = tile_key[:, first_col:first_col + E]
        value_head = tile_value[:, first_col:first_col + E]
        cot_head = out_cotangent[:, first_col:first_col + E]
        peaks = []
        totals = []
        numers = []
        for level_idx in range(LEVELS):
            stride = 2 ** level_idx
            offset = head_index % stride
            segments = TOKENS // (stride * TOK_DEV)
            q_seg = query_head[offset::stride].reshape(segments, TOK_DEV, E).astype(jnp.float32)
            k_seg = key_head[offset::stride].reshape(segments, TOK_DEV, E).astype(jnp.float32)
            v_seg = value_head[offset::stride].reshape(segments, TOK_DEV, E).astype(jnp.float32)
            scores = jnp.einsum("gqe,gke->gqk", q_seg, k_seg) * score_scale
            peak = jnp.max(scores, axis=-1)
            expo = jnp.exp(scores - peak[..., None])
            total = jnp.sum(expo, axis=-1)
            numer = jnp.einsum("gqk,gke->gqe", rounded(expo), v_seg)
            peaks.append(jnp.full((TOKENS,), NEG_FILL, jnp.float32).at[offset::stride].set(peak.reshape(-1)))
            totals.append(jnp.zeros((TOKENS,), jnp.float32).at[offset::stride].set(total.reshape(-1)))
            numers.append(jnp.zeros((TOKENS, E), jnp.float32).at[offset::stride].set(numer.reshape(-1, E)))
        top = jnp.max(jnp.stack(peaks), axis=0)
        factors = [jnp.exp(peak_row - top) for peak_row in peaks]
        norm = sum(total_row * factor for total_row, factor in zip(totals, factors))
        mixed = sum(numer_row * factor[:, None] for numer_row, factor in zip(numers, factors)) / norm[:, None]
        attended = mixed.astype(jnp.bfloat16)
        log_total = top + jnp.log(norm)
        delta = jnp.sum(cot_head.astype(jnp.float32) * attended.astype(jnp.float32), axis=-1)
        grad_q_acc = jnp.zeros((TOKENS, E), jnp.float32)
        grad_k_acc = jnp.zeros((TOKENS, E), jnp.float32)
        grad_v_acc = jnp.zeros((TOKENS, E), jnp.float32)
        for level_idx in range(LEVELS):
            stride = 2 ** level_idx
            offset = head_index % stride
            segments = TOKENS // (stride * TOK_DEV)
            q_seg = query_head[offset::stride].reshape(segments, TOK_DEV, E).astype(jnp.float32)
            k_seg = key_head[offset::stride].reshape(segments, TOK_DEV, E).astype(jnp.float32)
            v_seg = value_head[offset::stride].reshape(segments, TOK_DEV, E).astype(jnp.float32)
            c_seg = cot_head[offset::stride].reshape(segments, TOK_DEV, E).astype(jnp.float32)
            lse_seg = log_total[offset::stride].reshape(segments, TOK_DEV)
            delta_seg = delta[offset::stride].reshape(segments, TOK_DEV)
            scores = jnp.einsum("gqe,gke->gqk", q_seg, k_seg) * score_scale
            probs = jnp.exp(scores - lse_seg[..., None])
            dprob = jnp.einsum("gqe,gke->gqk", c_seg, v_seg)
            dscore = rounded(probs * (dprob - delta_seg[..., None]))
            grad_q_level = jnp.einsum("gqk,gke->gqe", dscore, k_seg) * score_scale
            grad_k_level = jnp.einsum("gqk,gqe->gke", dscore, q_seg) * score_scale
            grad_v_level = jnp.einsum("gqk,gqe->gke", rounded(probs), c_seg)
            grad_q_acc = grad_q_acc.at[offset::stride].add(grad_q_level.reshape(-1, E))
            grad_k_acc = grad_k_acc.at[offset::stride].add(grad_k_level.reshape(-1, E))
            grad_v_acc = grad_v_acc.at[offset::stride].add(grad_v_level.reshape(-1, E))
        out_cols.append(attended)
        gq_cols.append(grad_q_acc.astype(jnp.bfloat16))
        gk_cols.append(grad_k_acc.astype(jnp.bfloat16))
        gv_cols.append(grad_v_acc.astype(jnp.bfloat16))
    return (jnp.concatenate(out_cols, axis=1).T, jnp.concatenate(gq_cols, axis=1).T, jnp.concatenate(gk_cols, axis=1).T, jnp.concatenate(gv_cols, axis=1).T)
```

```python
import math

import jax
import jax.numpy as jnp
from jax import lax
from jax.experimental import pallas as pl
from jax.experimental.pallas import tpu as pltpu
from jax.sharding import PartitionSpec as P

E = 64
HEADS = 3
N = 512
W = HEADS * 128
F32 = jnp.float32
BF16 = jnp.bfloat16
NEG = -1e30
SCALE2 = math.log2(math.e) / math.sqrt(E)

Y0, X0, Z0, RROWS = 0, 512, 1024, 1536
Y_AT = {1: 0, 2: 256, 3: 384}
Y_ROWS = {1: 256, 2: 128, 3: 128}
X_AT = {4: 512, 8: 768, 12: 896}
X_ROWS = {4: 64, 8: 32, 12: 32}


def nn(a, b):
    return lax.dot_general(a, b, (((1,), (0,)), ((), ())), preferred_element_type=F32)


def nt(a, b):
    return lax.dot_general(a, b, (((1,), (1,)), ((), ())), preferred_element_type=F32)


def level_of(index):
    level = jnp.zeros(index.shape, jnp.int32)
    for bound in (8, 16, 32, 64, 128, 256):
        level = level + (index < bound).astype(jnp.int32)
    return level


def pad_lanes(x, value, lanes=N):
    if x.shape[1] == lanes:
        return x
    fill = jnp.full((x.shape[0], lanes - x.shape[1]), value, x.dtype)
    return jnp.concatenate([x, fill], axis=1)


def body(
    q_hbm, k_hbm, v_hbm, c_hbm, o_hbm, gq_hbm, gk_hbm, gv_hbm,
    xin, pt, own, d6, qc, xp, rq, rc, bias0, bias1, bias2,
    e0, dp0, e1, e2, num, dqa,
    rk, rkt, t32, t48, gsend, yacc, pacc, oacc, rx, rz, ry, ryz, rzz,
    ov, gqv, gkv, gvv,
    in_sem, out_sem, send_sem, recv_sem,
):
    me = lax.axis_index("seq")
    head0 = lax.axis_index("head") * HEADS
    z, x, y = lax.div(me, 16), lax.rem(lax.div(me, 4), 4), lax.rem(me, 4)

    def flipped(v, bits):
        if bits == 0:
            return v
        if bits == 1:
            return v + 1 - 2 * lax.rem(v, 2)
        if bits == 2:
            return lax.rem(v + 2, 4)
        return 3 - v

    peer = {e: flipped(z, e // 16) * 16 + flipped(x, e // 4 % 4) * 4 + flipped(y, e % 4)
            for e in (1, 2, 3, 4, 8, 12, 16, 32, 48)}

    loads = []
    for at, src in enumerate((k_hbm, v_hbm, q_hbm, c_hbm)):
        load = pltpu.make_async_copy(src, xin.at[:, pl.ds(64 * at, 64), :], in_sem.at[at])
        load.start()
        loads.append(load)
    barrier = pltpu.get_barrier_semaphore()
    for e in peer:
        pl.semaphore_signal(
            barrier, inc=1, device_id={"seq": peer[e]}, device_id_type=pl.DeviceIdType.MESH
        )

    started = []

    def send(src, dst, e):
        at = len(started)
        copy = pltpu.make_async_remote_copy(
            src_ref=src,
            dst_ref=dst,
            send_sem=send_sem.at[at],
            recv_sem=recv_sem.at[at],
            device_id={"seq": peer[e]},
            device_id_type=pl.DeviceIdType.MESH,
        )
        copy.start()
        started.append(copy)
        return copy

    place = lax.broadcasted_iota(jnp.int32, (N, 128), 0)
    lane = lax.broadcasted_iota(jnp.int32, (8, 128), 1)
    u = 64 * place
    for bits in range(4, 10):
        u = jnp.where(place >= 1 << (bits - 1), ((2 * place + 1) << (9 - bits)) & (N - 1), u)
    for h in range(HEADS):
        for t in range(4):
            tile = (lane + (128 * t + N) - (head0 + h)) & (N - 1)
            hot = u == jnp.broadcast_to(tile[0:1], (N, 128))
            pt[h, :, 128 * t : 128 * t + 128] = jnp.where(hot, 1.0, 0.0).astype(BF16)

    for load in loads:
        load.wait()
    low = lax.broadcasted_iota(jnp.int32, (N, 128), 1) < E
    for h in range(HEADS):
        hs = slice(128 * h, 128 * h + 128)
        rows = nt(pt[h], xin[h])
        own[:, hs] = rows[:, 0:128].astype(BF16)
        d6[:, hs] = jnp.concatenate([rows[0:8, 0:128]] * 2, axis=0).astype(BF16)
        right = rows[:, 128:256]
        qc[h, 0:N, :] = jnp.where(low, right, 0.0).astype(BF16)
        qc[h, N : 2 * N, :] = jnp.where(low, 0.0, right).astype(BF16)

    pl.semaphore_wait(barrier, len(peer))
    first = {}
    first[4] = send(own.at[0:64], rk.at[512:576], 4)
    first[8] = send(own.at[0:32], rk.at[768:800], 8)
    first[12] = send(own.at[0:32], rk.at[896:928], 12)
    first[16] = send(own.at[0:16], rk.at[1024:1040], 16)
    first[32] = send(d6, t32, 32)
    first[48] = send(d6, t48, 48)
    for e in (1, 2, 3):
        first[e] = send(own.at[0 : Y_ROWS[e]], rk.at[Y_AT[e] : Y_AT[e] + Y_ROWS[e]], e)

    def fill_bias(ref, at, rows, lanes, key_place, group):
        lq = level_of(lax.broadcasted_iota(jnp.int32, (rows, lanes), 1))
        mult = jnp.minimum(lq, level_of(key_place)) - (group - 1)
        value = jnp.where(mult > 0, jnp.log2(jnp.maximum(mult, 1).astype(F32)), NEG)
        ref[at : at + rows, :] = value

    r256 = lax.broadcasted_iota(jnp.int32, (256, 256), 0)
    fill_bias(bias0, 0, 256, 256, r256, 0)
    fill_bias(bias1, 0, 256, 256, r256, 1)
    r256 = lax.broadcasted_iota(jnp.int32, (256, 128), 0)
    fill_bias(bias2, 0, 256, 128, r256 & 127, 2)
    fill_bias(bias2, 256, 256, 128, r256 & 63, 3)
    fill_bias(bias2, 512, 256, 128, r256 & 31, 4)
    r512 = lax.broadcasted_iota(jnp.int32, (512, 128), 0)
    in_pack = r512 & 31
    fill_bias(
        bias2, 768, 512, 128, jnp.where(in_pack < 16, in_pack, 0), jnp.where(in_pack < 16, 5, 6)
    )

    zero = jnp.zeros((E, N), BF16)
    for h in range(HEADS):
        cols = nt(xin[h], pt[h]).astype(BF16)
        xp[h] = cols
        rq[h, 0:E, :] = cols[128:192]
        rq[h, E:128, :] = zero
        rc[h, 0:E, :] = zero
        rc[h, E:128, :] = cols[192:256]

    def attend(keys, queries, bias_value):
        score = nn(keys, queries) * SCALE2
        if bias_value is not None:
            score = score + bias_value
        peak = jnp.max(score, axis=0, keepdims=True)
        expo = jnp.exp2(score - peak)
        return peak, expo, jnp.sum(expo, axis=0, keepdims=True)

    peaks = [[] for _ in range(HEADS)]
    sums = [[] for _ in range(HEADS)]

    def local_forward(h):
        hs = slice(128 * h, 128 * h + 128)
        pieces = []
        for t in range(2):
            qs = slice(256 * t, 256 * t + 256)
            score = nn(own[:, hs], rq[h, :, qs]) * SCALE2
            if t == 0:
                score = jnp.concatenate([score[0:256] + bias0[...], score[256:512]], axis=0)
            peak = jnp.max(score, axis=0, keepdims=True)
            expo = jnp.exp2(score - peak)
            e0[h, :, qs] = expo
            num[h, :, qs] = nn(xp[h, 0:128, :], expo.astype(BF16))
            pieces.append((peak, jnp.sum(expo, axis=0, keepdims=True)))
        peaks[h].append(jnp.concatenate([p for p, _ in pieces], axis=1))
        sums[h].append(jnp.concatenate([s for _, s in pieces], axis=1))
        dp0[h] = nn(own[:, hs], rc[h])

    local_forward(0)

    for e in (16, 32, 48):
        first[e].wait_recv()
    rk[Z0 + 16 : Z0 + 32, :] = jnp.concatenate(
        [t32[...].astype(F32)[0:8], t48[...].astype(F32)[8:16]], axis=0
    ).astype(BF16)
    packs = {}
    for e in (1, 2, 3, 4, 8, 12):
        packs[e] = send(rk.at[Z0 : Z0 + 32], rk.at[Z0 + 32 * e : Z0 + 32 * e + 32], e)
    second = []
    for b in (1, 2, 3):
        first[b].wait_recv()
        for e in (4, 8, 12):
            n = X_ROWS[e]
            to = X_AT[e] + n * b
            second.append(send(rk.at[Y_AT[b] : Y_AT[b] + n], rk.at[to : to + n], e))

    local_forward(1)
    for b in (1, 2, 3):
        packs[b].wait_recv()
    for e in (4, 8, 12):
        to = Z0 + 32 * e + 32
        second.append(send(rk.at[Z0 + 32 : Z0 + 128], rk.at[to : to + 96], e))

    local_forward(2)

    nums1 = []
    nums2 = []
    for h in range(HEADS):
        hs = slice(128 * h, 128 * h + 128)
        rkt[h, :, 0:512] = rk[0:512, hs].T
        peak, expo, total = attend(rk[0:256, hs], rq[h, :, 0:256], bias1[...])
        e1[h] = expo
        nums1.append(nn(rkt[h, :, 0:256], expo.astype(BF16)))
        peaks[h].append(pad_lanes(peak, NEG))
        sums[h].append(pad_lanes(total, 0.0))

    for e in (4, 8, 12):
        first[e].wait_recv()
        packs[e].wait_recv()
    for copy in second:
        copy.wait_recv()

    delta = []
    gain = []
    for h in range(HEADS):
        hs = slice(128 * h, 128 * h + 128)
        rkt[h, :, 512:1536] = rk[512:1536, hs].T
        peak, expo, total = attend(rk[256:1536, hs], rq[h, :, 0:128], bias2[...])
        e2[h] = expo
        nums2.append(nn(rkt[h, :, 256:1536], expo.astype(BF16)))
        peaks[h].append(pad_lanes(peak, NEG))
        sums[h].append(pad_lanes(total, 0.0))

    for h in range(HEADS):
        top = jnp.maximum(jnp.maximum(peaks[h][0], peaks[h][1]), peaks[h][2])
        factor = [jnp.exp2(p - top) for p in peaks[h]]
        norm = sum(f * s for f, s in zip(factor, sums[h]))
        inv = 1.0 / norm
        gains = [f * inv for f in factor]
        mixed = (
            num[h] * gains[0]
            + pad_lanes(nums1[h] * gains[1][:, 0:256], 0.0)
            + pad_lanes(nums2[h] * gains[2][:, 0:128], 0.0)
        )
        attended = mixed[E:128].astype(BF16)
        cot = xp[h, 192:256, :].astype(F32)
        delta.append(jnp.sum(cot * attended.astype(F32), axis=0, keepdims=True))
        gain.append(gains)
        xp[h, 192:256, :] = attended

    def backward(h, keys, dprob, expo, g, nq):
        probs = expo * g[:, 0:nq]
        if dprob is None:
            dprob = nn(keys, rc[h, :, 0:nq])
        dscore = (probs * (dprob - delta[h][:, 0:nq])).astype(BF16)
        both = jnp.concatenate([dscore, probs.astype(BF16)], axis=1)
        right = jnp.concatenate([qc[h, 0:nq, :], qc[h, N : N + nq, :]], axis=0)
        return dscore, nn(both, right)

    for h in range(HEADS):
        hs = slice(128 * h, 128 * h + 128)
        dscore, dkv = backward(h, rk[512:1536, hs], None, e2[h, 256:1280, :], gain[h][2], 128)
        gsend[512:1024, hs] = dkv[0:512].astype(BF16)
        gsend[1152:1536, hs] = dkv[640:1024].astype(BF16)
        pacc[:, hs] = dkv[512:640]
        dqa[h, :, 0:128] = nn(rkt[h, :, 512:1536], dscore)
        dqa[h, :, 128:512] = jnp.zeros((128, 384), F32)
    hop_x = {}
    rx_at = {4: 0, 8: 256, 12: 384}
    rz_at = {4: 0, 8: 128, 12: 256}
    for e in (4, 8, 12):
        n = 4 * X_ROWS[e]
        hop_x[e] = (
            send(gsend.at[X_AT[e] : X_AT[e] + n], rx.at[rx_at[e] : rx_at[e] + n], e),
            send(gsend.at[Z0 + 32 * e : Z0 + 32 * e + 128], rz.at[rz_at[e] : rz_at[e] + 128], e),
        )

    for h in range(HEADS):
        hs = slice(128 * h, 128 * h + 128)
        dscore, dkv = backward(h, rk[0:256, hs], None, e1[h], gain[h][1], 256)
        dqa[h, :, 0:256] += nn(rkt[h, :, 0:256], dscore)
        yacc[0:64, hs] = dkv[0:64]
        gsend[64:256, hs] = dkv[64:256].astype(BF16)
        dscore, dkv = backward(h, rk[256:512, hs], None, e2[h, 0:256, :], gain[h][2], 128)
        dqa[h, :, 0:128] += nn(rkt[h, :, 256:512], dscore)
        yacc[64:128, hs] = dkv[0:64]
        gsend[320:384, hs] = dkv[64:128].astype(BF16)
        yacc[128:192, hs] = dkv[128:192]
        gsend[448:512, hs] = dkv[192:256].astype(BF16)
    ry_at = {1: 0, 2: 256, 3: 384}
    tails = []
    for e in (1, 2, 3):
        n = Y_ROWS[e] - 64
        a = Y_AT[e] + 64
        b = ry_at[e] + 64
        tails.append(send(gsend.at[a : a + n], ry.at[b : b + n], e))

    def local_backward(h):
        hs = slice(128 * h, 128 * h + 128)
        dscore, dkv = backward(h, None, dp0[h], e0[h], gain[h][0], N)
        oacc[:, hs] = dkv
        dqa[h] += nn(xp[h, 0:128, :], dscore)
        both = jnp.concatenate([xp[h, 192:256, :], dqa[h, 0:E, :].astype(BF16)], axis=0)
        done = nn(both, pt[h])
        ov[h] = done[0:E].astype(BF16)
        gqv[h] = (done[E:128] * 0.125).astype(BF16)

    local_backward(0)

    for e in (4, 8, 12):
        for copy in hop_x[e]:
            copy.wait_recv()
    heads_y = []
    packs_y = []
    for b in (1, 2, 3):
        part = yacc[64 * (b - 1) : 64 * b, :] + rx[64 * b : 64 * b + 64, :].astype(F32)
        small = rx[256 + 32 * b : 288 + 32 * b, :].astype(F32) + rx[
            384 + 32 * b : 416 + 32 * b, :
        ].astype(F32)
        gsend[Y_AT[b] : Y_AT[b] + 32, :] = (part[0:32] + small).astype(BF16)
        gsend[Y_AT[b] + 32 : Y_AT[b] + 64, :] = part[32:64].astype(BF16)
        pack = pacc[32 * b : 32 * b + 32, :]
        for e in (4, 8, 12):
            pack = pack + rz[rz_at[e] + 32 * b : rz_at[e] + 32 * b + 32, :].astype(F32)
        gsend[Z0 + 32 * b : Z0 + 32 * b + 32, :] = pack.astype(BF16)
        packs_y.append(
            send(gsend.at[Z0 + 32 * b : Z0 + 32 * b + 32], ryz.at[32 * (b - 1) : 32 * b], b)
        )
        heads_y.append(
            send(gsend.at[Y_AT[b] : Y_AT[b] + 64], ry.at[ry_at[b] : ry_at[b] + 64], b)
        )

    local_backward(1)

    for copy in packs_y:
        copy.wait_recv()
    pack = pacc[0:32, :]
    for e in (4, 8, 12):
        pack = pack + rz[rz_at[e] : rz_at[e] + 32, :].astype(F32)
    for b in (1, 2, 3):
        pack = pack + ryz[32 * (b - 1) : 32 * b, :].astype(F32)
    gsend[Z0 : Z0 + 32, :] = pack.astype(BF16)
    hop_z = [
        send(gsend.at[Z0 : Z0 + 16], rzz.at[0:16], 16),
        send(gsend.at[Z0 + 16 : Z0 + 32], rzz.at[16:32], 32),
        send(gsend.at[Z0 + 16 : Z0 + 32], rzz.at[32:48], 48),
    ]

    local_backward(2)
    stores = [
        pltpu.make_async_copy(ov, o_hbm, out_sem.at[0]),
        pltpu.make_async_copy(gqv, gq_hbm, out_sem.at[1]),
    ]
    for store in stores:
        store.start()

    for copy in tails + heads_y + hop_z:
        copy.wait_recv()
    for h in range(HEADS):
        hs = slice(128 * h, 128 * h + 128)
        a = oacc[0:64, hs] + rx[0:64, hs].astype(F32)
        for b in (1, 2, 3):
            a = a + ry[ry_at[b] : ry_at[b] + 64, hs].astype(F32)
        a32 = a[0:32] + rx[256:288, hs].astype(F32) + rx[384:416, hs].astype(F32)
        a16 = a32[0:16] + rzz[0:16, hs].astype(F32)
        a8 = a16[0:8] + rzz[16:32, hs].astype(F32)[0:8] + rzz[32:48, hs].astype(F32)[8:16]
        b128 = oacc[64:128, hs]
        for b in (1, 2, 3):
            b128 = b128 + ry[ry_at[b] + 64 : ry_at[b] + 128, hs].astype(F32)
        b256 = oacc[128:256, hs] + ry[128:256, hs].astype(F32)
        whole = jnp.concatenate(
            [a8, a16[8:16], a32[16:32], a[32:64], b128, b256, oacc[256:512, hs]], axis=0
        )
        done = nn(whole.T.astype(BF16), pt[h])
        gkv[h] = (done[0:E] * 0.125).astype(BF16)
        gvv[h] = done[E:128].astype(BF16)
    last = [
        pltpu.make_async_copy(gkv, gk_hbm, out_sem.at[2]),
        pltpu.make_async_copy(gvv, gv_hbm, out_sem.at[3]),
    ]
    for store in last:
        store.start()
    for copy in started:
        copy.wait_send()
    for store in stores + last:
        store.wait()


COPIES = 45


def per_device(tile_query, tile_key, tile_value, out_cotangent):
    shape = (HEADS, E, N)
    args = [a.reshape(shape) for a in (tile_query, tile_key, tile_value, out_cotangent)]
    vm = pltpu.VMEM
    outs = pl.pallas_call(
        body,
        out_shape=[jax.ShapeDtypeStruct(shape, BF16)] * 4,
        in_specs=[pl.BlockSpec(memory_space=pl.ANY)] * 4,
        out_specs=[pl.BlockSpec(memory_space=pl.ANY)] * 4,
        scratch_shapes=[
            vm((HEADS, 256, N), BF16),
            vm((HEADS, N, N), BF16),
            vm((N, W), BF16),
            vm((16, W), BF16),
            vm((HEADS, 2 * N, 128), BF16),
            vm((HEADS, 256, N), BF16),
            vm((HEADS, 128, N), BF16),
            vm((HEADS, 128, N), BF16),
            vm((256, 256), F32),
            vm((256, 256), F32),
            vm((1280, 128), F32),
            vm((HEADS, N, N), F32),
            vm((HEADS, N, N), F32),
            vm((HEADS, 256, 256), F32),
            vm((HEADS, 1280, 128), F32),
            vm((HEADS, 128, N), F32),
            vm((HEADS, 128, N), F32),
            vm((RROWS, W), BF16),
            vm((HEADS, 128, RROWS), BF16),
            vm((16, W), BF16),
            vm((16, W), BF16),
            vm((RROWS, W), BF16),
            vm((192, W), F32),
            vm((128, W), F32),
            vm((N, W), F32),
            vm((512, W), BF16),
            vm((384, W), BF16),
            vm((512, W), BF16),
            vm((96, W), BF16),
            vm((48, W), BF16),
            vm(shape, BF16),
            vm(shape, BF16),
            vm(shape, BF16),
            vm(shape, BF16),
            pltpu.SemaphoreType.DMA((4,)),
            pltpu.SemaphoreType.DMA((4,)),
            pltpu.SemaphoreType.DMA((COPIES,)),
            pltpu.SemaphoreType.DMA((COPIES,)),
        ],
        compiler_params=pltpu.CompilerParams(
            collective_id=0, has_side_effects=True, vmem_limit_bytes=56 * 2**20
        ),
        name="dilated",
    )(*args)
    return tuple(o.reshape(HEADS * E, N) for o in outs)


def solution(mesh):
    spec = P("head", "seq")
    return jax.shard_map(
        per_device, mesh=mesh, in_specs=(spec,) * 4, out_specs=(spec,) * 4, check_vma=False
    )
```

```python
import math

import jax
import jax.numpy as jnp
from jax import lax
from jax.experimental import pallas as pl
from jax.experimental.pallas import tpu as pltpu
from jax.sharding import PartitionSpec as P

E = 64
HEADS = 3
N = 512
W = HEADS * 128
F32 = jnp.float32
BF16 = jnp.bfloat16
NEG = -1e30
SCALE2 = math.log2(math.e) / math.sqrt(E)

ROWS = 1536
Y_AT, Y_ROWS = {1: 0, 2: 256, 3: 384}, {1: 256, 2: 128, 3: 128}
X_AT, X_ROWS = {4: 512, 8: 768, 12: 896}, {4: 64, 8: 32, 12: 32}
S5, S6 = 1024, 1280


def slot_at(d):
    return X_AT[d // 4 * 4] + X_ROWS[d // 4 * 4] * (d % 4)


def nn(a, b):
    return lax.dot_general(a, b, (((1,), (0,)), ((), ())), preferred_element_type=F32)


def nt(a, b):
    return lax.dot_general(a, b, (((1,), (1,)), ((), ())), preferred_element_type=F32)


def level_of(index):
    level = jnp.zeros(index.shape, jnp.int32)
    for bound in (8, 16, 32, 64, 128, 256):
        level = level + (index < bound).astype(jnp.int32)
    return level


def body(
    q_hbm, k_hbm, v_hbm, c_hbm, out,
    xin, pt, own, d6, qc, xp, rq, rc, bias0, bias1, bias2,
    e0, dp0, e1, dp1, e2, dp2, num, nums, dqa, early,
    rk, rkt, t32, t48, gsend, yacc, xacc, pacc, oacc,
    rx0, rx12, r3, rz5, rz6, ry, pz, ryz, rzz,
    in_sem, send_sem, recv_sem,
):
    me = lax.axis_index("seq")
    head0 = lax.axis_index("head") * HEADS
    z, x, y = lax.div(me, 16), lax.rem(lax.div(me, 4), 4), lax.rem(me, 4)

    def flipped(v, bits):
        if bits == 0:
            return v
        if bits == 1:
            return v + 1 - 2 * lax.rem(v, 2)
        if bits == 2:
            return lax.rem(v + 2, 4)
        return 3 - v

    peer = {e: flipped(z, e // 16) * 16 + flipped(x, e // 4 % 4) * 4 + flipped(y, e % 4)
            for e in (1, 2, 3, 4, 8, 12, 16, 32, 48)}

    loads = []
    for at, src in enumerate((k_hbm, v_hbm, q_hbm, c_hbm)):
        load = pltpu.make_async_copy(src, xin.at[:, pl.ds(64 * at, 64), :], in_sem.at[at])
        load.start()
        loads.append(load)
    barrier = pltpu.get_barrier_semaphore()
    for e in peer:
        pl.semaphore_signal(
            barrier, inc=1, device_id={"seq": peer[e]}, device_id_type=pl.DeviceIdType.MESH
        )

    copies, landed = {}, set()

    def send(key, src, dst, e):
        at = len(copies)
        copies[key] = pltpu.make_async_remote_copy(
            src_ref=src,
            dst_ref=dst,
            send_sem=send_sem.at[at],
            recv_sem=recv_sem.at[at],
            device_id={"seq": peer[e]},
            device_id_type=pl.DeviceIdType.MESH,
        )
        copies[key].start()

    def need(*keys):
        for key in keys:
            if key not in landed:
                copies[key].wait_recv()
                landed.add(key)

    def move(key, e, src, a, dst, b, n):
        send(key, src.at[a : a + n], dst.at[b : b + n], e)

    def head_lanes(h):
        return slice(128 * h, 128 * h + 128)

    place = lax.broadcasted_iota(jnp.int32, (N, 128), 0)
    lane = lax.broadcasted_iota(jnp.int32, (8, 128), 1)
    u = 64 * place
    for bits in range(4, 10):
        u = jnp.where(place >= 1 << (bits - 1), ((2 * place + 1) << (9 - bits)) & (N - 1), u)
    for h in range(HEADS):
        for t in range(4):
            tile = (lane + (128 * t + N) - (head0 + h)) & (N - 1)
            hot = u == jnp.broadcast_to(tile[0:1], (N, 128))
            pt[h, :, 128 * t : 128 * t + 128] = jnp.where(hot, 1.0, 0.0).astype(BF16)

    for load in loads[0:2]:
        load.wait()
    for h in range(HEADS):
        rows = nt(pt[h], xin[h, 0:128, :])
        own[:, head_lanes(h)] = rows.astype(BF16)
        d6[:, head_lanes(h)] = jnp.concatenate([rows[0:8]] * 2, axis=0).astype(BF16)

    pl.semaphore_wait(barrier, len(peer))
    move("x4_0", 4, own, 0, rk, slot_at(4), 64)
    move("ya1", 1, own, 0, rk, Y_AT[1], 64)
    send("z32", d6, t32, 32)
    send("z48", d6, t48, 48)
    move("ya3", 3, own, 0, rk, Y_AT[3], 64)
    move("x8_0", 8, own, 0, rk, slot_at(8), 32)
    move("ya2", 2, own, 0, rk, Y_AT[2], 64)
    move("x12_0", 12, own, 0, rk, slot_at(12), 32)
    move("zl0", 16, own, 0, rk, S5, 16)

    for load in loads[2:4]:
        load.wait()
    low = lax.broadcasted_iota(jnp.int32, (N, 128), 1) < E
    zero = jnp.zeros((E, N), BF16)
    for h in range(HEADS):
        right = nt(pt[h], xin[h, 128:256, :])
        qc[h, 0:N, :] = jnp.where(low, right, 0.0).astype(BF16)
        qc[h, N : 2 * N, :] = jnp.where(low, 0.0, right).astype(BF16)
        cols = nt(xin[h], pt[h]).astype(BF16)
        xp[h] = cols
        rq[h, 0:E, :] = cols[128:192]
        rq[h, E:128, :] = zero
        rc[h, 0:E, :] = zero
        rc[h, E:128, :] = cols[192:256]

    def fill_bias(ref, at, rows, lanes, key_place, group):
        lq = level_of(lax.broadcasted_iota(jnp.int32, (rows, lanes), 1))
        mult = jnp.minimum(lq, level_of(key_place)) - (group - 1)
        value = jnp.where(mult > 0, jnp.log2(jnp.maximum(mult, 1).astype(F32)), NEG)
        ref[at : at + rows, :] = value

    wide = lax.broadcasted_iota(jnp.int32, (256, 256), 0)
    r256 = lax.broadcasted_iota(jnp.int32, (256, 128), 0)
    fill_bias(bias0, 0, 256, 256, wide, 0)

    def forward(score, values):
        peak = jnp.max(score, axis=0, keepdims=True)
        expo = jnp.exp2(score - peak)
        total = jnp.sum(expo, axis=0, keepdims=True)
        return peak, expo, total, nn(values, expo.astype(BF16))[E:128]

    local = [[] for _ in range(HEADS)]
    part1 = [None] * HEADS
    parts2 = [[] for _ in range(HEADS)]

    def local_forward(h):
        for t in range(2):
            qs = slice(256 * t, 256 * t + 256)
            score = nn(own[:, head_lanes(h)], rq[h, :, qs]) * SCALE2
            if t == 0:
                score = jnp.concatenate([score[0:256] + bias0[...], score[256:512]], axis=0)
            peak, expo, total, mix = forward(score, xp[h, 0:128, :])
            e0[h, :, qs] = expo
            num[h, :, qs] = mix
            local[h].append((peak, total))

    def remote_forward(h, a, b):
        ks = slice(256 + a, 256 + b)
        keys = rk[ks, head_lanes(h)]
        rkt[h, :, ks] = keys.T
        dp2[h, a:b, :] = nn(keys, rc[h, :, 0:128])
        score = nn(keys, rq[h, :, 0:128]) * SCALE2 + bias2[a:b, :]
        peak, expo, total, mix = forward(score, rkt[h, :, ks])
        e2[h, a:b, :] = expo
        at = 256 + 128 * len(parts2[h])
        nums[h, :, at : at + 128] = mix
        parts2[h].append((peak, total, at, a, b))

    local_forward(0)

    need("z32", "z48")
    rk[S6 : S6 + 16, :] = jnp.concatenate(
        [t32[...].astype(F32)[0:8], t48[...].astype(F32)[8:16]], axis=0
    ).astype(BF16)
    for e in (1, 2, 3, 4, 8, 12):
        move(f"p{e}", e, rk, S6, rk, S6 + 16 * e, 16)
    for b in (1, 2):
        need(f"ya{b}")
        for e in (4, 8, 12):
            move(f"x{e}_{b}", e, rk, Y_AT[b], rk, slot_at(e + b), X_ROWS[e])
    for e in (4, 12, 8):
        need(f"x{e}_0")
        move(f"x{e}_3", 3, rk, slot_at(e), rk, slot_at(e + 3), X_ROWS[e])
    move("yb1", 1, own, 64, rk, Y_AT[1] + 64, 192)
    move("yb3", 3, own, 64, rk, Y_AT[3] + 64, 64)
    move("yb2", 2, own, 64, rk, Y_AT[2] + 64, 64)

    def last_z(*slots):
        for d in slots:
            src = Y_AT[d] if d < 4 else slot_at(d)
            move(f"zl{d}", 16, rk, src, rk, S5 + 16 * d, 16)

    need("ya3")
    last_z(1, 2, 3, 4, 8, 12)

    local_forward(1)
    need("p1", "p2", "p3")
    for e in (4, 8, 12):
        move(f"pp{e}", e, rk, S6 + 16, rk, S6 + 16 * e + 16, 48)
    for e in (4, 12, 8):
        need(f"x{e}_1")
        last_z(e + 1)
    for e in (4, 12, 8):
        need(f"x{e}_2")
        last_z(e + 2)
    for e in (4, 12, 8):
        need(f"x{e}_3")
        last_z(e + 3)

    local_forward(2)
    fill_bias(bias2, 256, 256, 128, r256 & 63, 3)
    fill_bias(bias2, 512, 256, 128, r256 & 31, 4)
    fill_bias(bias2, 768, 256, 128, r256 & 15, 5)
    fill_bias(bias2, 1024, 256, 128, r256 & 7, 6)
    for h in range(HEADS):
        remote_forward(h, 256, 768)
    fill_bias(bias1, 0, 256, 256, wide, 1)
    fill_bias(bias2, 0, 256, 128, r256 & 127, 2)
    for h in range(HEADS):
        dp0[h] = nn(own[:, head_lanes(h)], rc[h])
    need("yb1", "yb2", "yb3")
    for h in range(HEADS):
        keys = rk[0:256, head_lanes(h)]
        rkt[h, :, 0:256] = keys.T
        dp1[h] = nn(keys, rc[h, :, 0:256])
        score = nn(keys, rq[h, :, 0:256]) * SCALE2 + bias1[...]
        peak, expo, total, mix = forward(score, rkt[h, :, 0:256])
        e1[h] = expo
        nums[h, :, 0:256] = mix
        part1[h] = (peak, total)
        remote_forward(h, 0, 256)
    for e in (4, 8, 12):
        need(f"p{e}", f"pp{e}")
    need(*(f"zl{d}" for d in range(16)))
    for h in range(HEADS):
        remote_forward(h, 768, 1280)

    def combine(h, lo, hi):
        t = lo // 256
        ls = slice(lo - 256 * t, hi - 256 * t)
        pieces = [(local[h][t][0][:, ls], local[h][t][1][:, ls], num[h, :, lo:hi])]
        if hi <= 256:
            pieces.append((part1[h][0][:, lo:hi], part1[h][1][:, lo:hi], nums[h, :, lo:hi]))
        if hi <= 128:
            for peak, total, at, _, _ in parts2[h]:
                pieces.append((peak, total, nums[h, :, at : at + 128]))
        top = pieces[0][0]
        for peak, _, _ in pieces[1:]:
            top = jnp.maximum(top, peak)
        factors = [jnp.exp2(peak - top) for peak, _, _ in pieces]
        inv = 1.0 / sum(f * total for f, (_, total, _) in zip(factors, pieces))
        gains = [f * inv for f in factors]
        attended = sum(g * mix for g, (_, _, mix) in zip(gains, pieces)).astype(BF16)
        cot = xp[h, 192:256, lo:hi].astype(F32)
        delta = jnp.sum(cot * attended.astype(F32), axis=0, keepdims=True)
        xp[h, 192:256, lo:hi] = attended
        return gains, delta

    def backward(h, dprob, expo, gain, delta, nq):
        probs = expo * gain
        dscore = (probs * (dprob - delta)).astype(BF16)
        both = jnp.concatenate([dscore, probs.astype(BF16)], axis=1)
        right = jnp.concatenate([qc[h, 0:nq, :], qc[h, N : N + nq, :]], axis=0)
        return dscore, nn(both, right)

    def remote_backward(h, which):
        _, _, _, a, b = parts2[h][which]
        gains, delta = first[h]
        dscore, dkv = backward(h, dp2[h, a:b, :], e2[h, a:b, :], gains[2 + which], delta, 128)
        return nn(rkt[h, :, 256 + a : 256 + b], dscore)[0:E], dkv

    first = [combine(h, 0, 128) for h in range(HEADS)]
    for h in range(HEADS):
        hs = head_lanes(h)
        dq, dkv = remote_backward(h, 0)
        gsend[512:1024, hs] = dkv.astype(BF16)
        xacc[0:64, hs] = dkv[0:64]
        xacc[64:96, hs] = dkv[256:288]
        xacc[96:128, hs] = dkv[384:416]
        dqz, dkv = remote_backward(h, 2)
        gsend[1024:1536, hs] = dkv.astype(BF16)
        pacc[0:64, hs] = dkv[0:64]
        pacc[64:128, hs] = dkv[256:320]
        dqa[h, :, 0:128] = dq + dqz
        dqa[h, :, 128:256] = jnp.zeros((E, 128), F32)
    r3_at = {4: 0, 8: 64, 12: 96}
    for e in (4, 8, 12):
        move(f"g{e}_3", 3, gsend, slot_at(e + 3), r3, r3_at[e], X_ROWS[e])
    z_at = {4: 0, 8: 64, 12: 128}
    x12_at = {4: 0, 8: 128, 12: 192}
    for e in (4, 8, 12):
        move(f"gp5{e}", e, gsend, S5 + 16 * e, rz5, z_at[e], 64)
        move(f"gp6{e}", e, gsend, S6 + 16 * e, rz6, z_at[e], 64)
    for e in (4, 8, 12):
        move(f"g{e}_12", e, gsend, slot_at(e + 1), rx12, x12_at[e], 2 * X_ROWS[e])

    second = [combine(h, 128, 256) for h in range(HEADS)]
    third = [combine(h, 256, 512) for h in range(HEADS)]
    delta_all = []
    for h in range(HEADS):
        hs = head_lanes(h)
        delta_all.append(jnp.concatenate([first[h][1], second[h][1], third[h][1]], axis=1))
        gain = jnp.concatenate([first[h][0][1], second[h][0][1]], axis=1)
        dscore, dkv = backward(h, dp1[h], e1[h], gain, delta_all[h][:, 0:256], 256)
        dqa[h, :, 0:256] += nn(rkt[h, :, 0:256], dscore)[0:E]
        yacc[0:64, hs] = dkv[0:64]
        gsend[64:256, hs] = dkv[64:256].astype(BF16)
        dq, dkv = remote_backward(h, 1)
        dqa[h, :, 0:128] += dq
        yacc[64:128, hs] = dkv[0:64]
        gsend[320:512, hs] = dkv[64:256].astype(BF16)
    move("gy3", 3, gsend, 384, ry, 384, 128)
    move("gy1", 1, gsend, 64, ry, 64, 192)
    move("gy2", 2, gsend, 320, ry, 320, 64)

    x0_at = {4: 0, 8: 64, 12: 96}
    for e in (4, 8, 12):
        n, at = X_ROWS[e], x0_at[e]
        need(f"g{e}_3")
        total = xacc[at : at + n, :] + r3[at : at + n, :].astype(F32)
        gsend[slot_at(e) : slot_at(e) + n, :] = total.astype(BF16)
        move(f"g{e}_0", e, gsend, slot_at(e), rx0, at, n)

    def local_backward(h):
        gain = jnp.concatenate([first[h][0][0], second[h][0][0], third[h][0][0]], axis=1)
        dscore, dkv = backward(h, dp0[h], e0[h], gain, delta_all[h], N)
        oacc[:, head_lanes(h)] = dkv
        dq = nn(xp[h, 0:128, :], dscore)[0:E]
        dq = jnp.concatenate([dq[:, 0:256] + dqa[h], dq[:, 256:512]], axis=1)
        done = nn(jnp.concatenate([xp[h, 192:256, :], dq.astype(BF16)], axis=0), pt[h])
        out[0, h] = done[0:E].astype(BF16)
        out[1, h] = (done[E:128] * 0.125).astype(BF16)

    local_backward(0)

    for e in (4, 8, 12):
        need(f"gp5{e}", f"gp6{e}")
    for b in (1, 2, 3):
        bs = slice(16 * b, 16 * b + 16)
        for part, got in ((0, rz5), (1, rz6)):
            total = pacc[64 * part + 16 * b : 64 * part + 16 * b + 16, :]
            for e in (4, 8, 12):
                total = total + got[z_at[e] + 16 * b : z_at[e] + 16 * b + 16, :].astype(F32)
            at = 32 * (b - 1) + 16 * part
            pz[at : at + 16, :] = total.astype(BF16)
        move(f"gpy{b}", b, pz, 32 * (b - 1), ryz, 32 * (b - 1), 32)
    for e in (4, 8, 12):
        need(f"g{e}_12")
    for b in (1, 2):
        part = yacc[64 * (b - 1) : 64 * b, :] + rx12[64 * (b - 1) : 64 * b, :].astype(F32)
        small = rx12[96 + 32 * b : 128 + 32 * b, :].astype(F32) + rx12[
            160 + 32 * b : 192 + 32 * b, :
        ].astype(F32)
        gsend[Y_AT[b] : Y_AT[b] + 32, :] = (part[0:32] + small).astype(BF16)
        gsend[Y_AT[b] + 32 : Y_AT[b] + 64, :] = part[32:64].astype(BF16)
        move(f"gya{b}", b, gsend, Y_AT[b], ry, Y_AT[b], 64)

    local_backward(1)

    need("gpy1", "gpy2", "gpy3")
    for part, got in ((0, rz5), (1, rz6)):
        total = pacc[64 * part : 64 * part + 16, :]
        for e in (4, 8, 12):
            total = total + got[z_at[e] : z_at[e] + 16, :].astype(F32)
        for b in (0, 1, 2):
            total = total + ryz[32 * b + 16 * part : 32 * b + 16 * part + 16, :].astype(F32)
        gsend[S5 + 256 * part : S5 + 256 * part + 16, :] = total.astype(BF16)
    move("gz16", 16, gsend, S5, rzz, 0, 16)
    move("gz32", 32, gsend, S6, rzz, 16, 16)
    move("gz48", 48, gsend, S6, rzz, 32, 16)

    local_backward(2)

    need("gy1", "gy2", "gy3")
    for h in range(HEADS):
        hs = head_lanes(h)
        b256 = oacc[128:256, hs] + ry[128:256, hs].astype(F32)
        whole = jnp.concatenate([b256, oacc[256:512, hs]], axis=0)
        early[h] = nn(whole.T.astype(BF16), pt[h, 128:512, :])
        b128 = oacc[64:128, hs]
        for b in (1, 2, 3):
            b128 = b128 + ry[Y_AT[b] + 64 : Y_AT[b] + 128, hs].astype(F32)
        oacc[64:128, hs] = b128

    need("g4_0", "g8_0", "g12_0", "gya1", "gya2", "gz16", "gz32", "gz48")
    for h in range(HEADS):
        hs = head_lanes(h)
        a = oacc[0:64, hs] + rx0[0:64, hs].astype(F32)
        for b in (1, 2, 3):
            a = a + ry[Y_AT[b] : Y_AT[b] + 64, hs].astype(F32)
        a32 = a[0:32] + rx0[64:96, hs].astype(F32) + rx0[96:128, hs].astype(F32)
        a16 = a32[0:16] + rzz[0:16, hs].astype(F32)
        a8 = a16[0:8] + rzz[16:32, hs].astype(F32)[0:8] + rzz[32:48, hs].astype(F32)[8:16]
        whole = jnp.concatenate([a8, a16[8:16], a32[16:32], a[32:64], oacc[64:128, hs]], axis=0)
        done = early[h] + nn(whole.T.astype(BF16), pt[h, 0:128, :])
        out[2, h] = (done[0:E] * 0.125).astype(BF16)
        out[3, h] = done[E:128].astype(BF16)
    for copy in copies.values():
        copy.wait_send()


def hand_out(res, o_hbm, gq_hbm, gk_hbm, gv_hbm, sem):
    moves = [
        pltpu.make_async_copy(res.at[at], dst, sem.at[at])
        for at, dst in enumerate((o_hbm, gq_hbm, gk_hbm, gv_hbm))
    ]
    for move in moves:
        move.start()
    for move in moves:
        move.wait()


COPIES = 72


def per_device(tile_query, tile_key, tile_value, out_cotangent):
    shape = (HEADS, E, N)
    args = [a.reshape(shape) for a in (tile_query, tile_key, tile_value, out_cotangent)]
    vm = pltpu.VMEM
    anywhere = pl.BlockSpec(memory_space=pl.ANY)
    res = pl.pallas_call(
        body,
        out_shape=jax.ShapeDtypeStruct((4, *shape), BF16),
        in_specs=[pl.BlockSpec(memory_space=pltpu.HBM)] * 4,
        out_specs=pl.BlockSpec(memory_space=pltpu.VMEM),
        scratch_shapes=[
            vm((HEADS, 256, N), BF16),
            vm((HEADS, N, N), BF16),
            vm((N, W), BF16),
            vm((16, W), BF16),
            vm((HEADS, 2 * N, 128), BF16),
            vm((HEADS, 256, N), BF16),
            vm((HEADS, 128, N), BF16),
            vm((HEADS, 128, N), BF16),
            vm((256, 256), F32),
            vm((256, 256), F32),
            vm((1280, 128), F32),
            vm((HEADS, N, N), F32),
            vm((HEADS, N, N), F32),
            vm((HEADS, 256, 256), F32),
            vm((HEADS, 256, 256), F32),
            vm((HEADS, 1280, 128), F32),
            vm((HEADS, 1280, 128), F32),
            vm((HEADS, E, N), F32),
            vm((HEADS, E, 640), F32),
            vm((HEADS, E, 256), F32),
            vm((HEADS, 128, N), F32),
            vm((ROWS, W), BF16),
            vm((HEADS, 128, ROWS), BF16),
            vm((16, W), BF16),
            vm((16, W), BF16),
            vm((ROWS, W), BF16),
            vm((128, W), F32),
            vm((128, W), F32),
            vm((128, W), F32),
            vm((N, W), F32),
            vm((128, W), BF16),
            vm((256, W), BF16),
            vm((128, W), BF16),
            vm((192, W), BF16),
            vm((192, W), BF16),
            vm((512, W), BF16),
            vm((96, W), BF16),
            vm((96, W), BF16),
            vm((48, W), BF16),
            pltpu.SemaphoreType.DMA((4,)),
            pltpu.SemaphoreType.DMA((COPIES,)),
            pltpu.SemaphoreType.DMA((COPIES,)),
        ],
        compiler_params=pltpu.CompilerParams(
            collective_id=0, has_side_effects=True, vmem_limit_bytes=44 * 2**20
        ),
        name="dilated",
    )(*args)
    outs = pl.pallas_call(
        hand_out,
        out_shape=[jax.ShapeDtypeStruct((HEADS * E, N), BF16)] * 4,
        in_specs=[anywhere],
        out_specs=[anywhere] * 4,
        scratch_shapes=[pltpu.SemaphoreType.DMA((4,))],
        compiler_params=pltpu.CompilerParams(vmem_limit_bytes=2**20),
        name="outputs",
    )(res.reshape(4, HEADS * E, N))
    return tuple(outs)


def solution(mesh):
    spec = P("head", "seq")
    return jax.shard_map(
        per_device, mesh=mesh, in_specs=(spec,) * 4, out_specs=(spec,) * 4, check_vma=False
    )
```

```python
import math

import jax
import jax.numpy as jnp
from jax import lax
from jax.experimental import pallas as pl
from jax.experimental.pallas import tpu as pltpu
from jax.sharding import PartitionSpec as P

E = 64
HEADS = 3
N = 512
W = HEADS * 128
F32 = jnp.float32
BF16 = jnp.bfloat16
NEG = -1e30
SCALE2 = math.log2(math.e) / math.sqrt(E)

ROWS = 1536
Y_AT, Y_ROWS = {1: 0, 2: 256, 3: 384}, {1: 256, 2: 128, 3: 128}
X_AT, X_ROWS = {4: 512, 8: 768, 12: 896}, {4: 64, 8: 32, 12: 32}
S5, S6 = 1024, 1280


def slot_at(d):
    return X_AT[d // 4 * 4] + X_ROWS[d // 4 * 4] * (d % 4)


def nn(a, b):
    return lax.dot_general(a, b, (((1,), (0,)), ((), ())), preferred_element_type=F32)


def nt(a, b):
    return lax.dot_general(a, b, (((1,), (1,)), ((), ())), preferred_element_type=F32)


def level_of(index):
    level = jnp.zeros(index.shape, jnp.int32)
    for bound in (8, 16, 32, 64, 128, 256):
        level = level + (index < bound).astype(jnp.int32)
    return level


def body(
    q_hbm, k_hbm, v_hbm, c_hbm, out_hbm,
    out,
    xin, pt, own, d6, qc, xp, rq, rc, bias0, bias1, bias2,
    e0, dp0, e1, dp1, e2, dp2, num, nums, dqa, early,
    rk, rkt, t32, t48, gsend, yacc, xacc, pacc, oacc,
    rx0, rx12, r3, rz5, rz6, ry, pz, ryz, rzz,
    in_sem, out_sem, send_sem, recv_sem,
):
    me = lax.axis_index("seq")
    head0 = lax.axis_index("head") * HEADS
    z, x, y = lax.div(me, 16), lax.rem(lax.div(me, 4), 4), lax.rem(me, 4)

    def flipped(v, bits):
        if bits == 0:
            return v
        if bits == 1:
            return v + 1 - 2 * lax.rem(v, 2)
        if bits == 2:
            return lax.rem(v + 2, 4)
        return 3 - v

    peer = {e: flipped(z, e // 16) * 16 + flipped(x, e // 4 % 4) * 4 + flipped(y, e % 4)
            for e in (1, 2, 3, 4, 8, 12, 16, 32, 48)}

    loads = []
    for at, src in enumerate((k_hbm, v_hbm, q_hbm, c_hbm)):
        load = pltpu.make_async_copy(src, xin.at[:, pl.ds(64 * at, 64), :], in_sem.at[at])
        load.start()
        loads.append(load)
    barrier = pltpu.get_barrier_semaphore()
    for e in peer:
        pl.semaphore_signal(
            barrier, inc=1, device_id={"seq": peer[e]}, device_id_type=pl.DeviceIdType.MESH
        )

    copies, landed = {}, set()

    def send(key, src, dst, e):
        at = len(copies)
        copies[key] = pltpu.make_async_remote_copy(
            src_ref=src,
            dst_ref=dst,
            send_sem=send_sem.at[at],
            recv_sem=recv_sem.at[at],
            device_id={"seq": peer[e]},
            device_id_type=pl.DeviceIdType.MESH,
        )
        copies[key].start()

    def need(*keys):
        for key in keys:
            if key not in landed:
                copies[key].wait_recv()
                landed.add(key)

    def move(key, e, src, a, dst, b, n):
        send(key, src.at[a : a + n], dst.at[b : b + n], e)

    def head_lanes(h):
        return slice(128 * h, 128 * h + 128)

    place = lax.broadcasted_iota(jnp.int32, (N, 128), 0)
    lane = lax.broadcasted_iota(jnp.int32, (8, 128), 1)
    u = 64 * place
    for bits in range(4, 10):
        u = jnp.where(place >= 1 << (bits - 1), ((2 * place + 1) << (9 - bits)) & (N - 1), u)
    for h in range(HEADS):
        for t in range(4):
            tile = (lane + (128 * t + N) - (head0 + h)) & (N - 1)
            hot = u == jnp.broadcast_to(tile[0:1], (N, 128))
            pt[h, :, 128 * t : 128 * t + 128] = jnp.where(hot, 1.0, 0.0).astype(BF16)

    for load in loads[0:2]:
        load.wait()
    for h in range(HEADS):
        rows = nt(pt[h], xin[h, 0:128, :])
        own[:, head_lanes(h)] = rows.astype(BF16)
        d6[:, head_lanes(h)] = jnp.concatenate([rows[0:8]] * 2, axis=0).astype(BF16)

    pl.semaphore_wait(barrier, len(peer))
    move("x4_0", 4, own, 0, rk, slot_at(4), 64)
    move("ya1", 1, own, 0, rk, Y_AT[1], 64)
    send("z32", d6, t32, 32)
    send("z48", d6, t48, 48)
    move("ya3", 3, own, 0, rk, Y_AT[3], 64)
    move("x8_0", 8, own, 0, rk, slot_at(8), 32)
    move("ya2", 2, own, 0, rk, Y_AT[2], 64)
    move("x12_0", 12, own, 0, rk, slot_at(12), 32)
    move("zl0", 16, own, 0, rk, S5, 16)

    for load in loads[2:4]:
        load.wait()
    low = lax.broadcasted_iota(jnp.int32, (N, 128), 1) < E
    zero = jnp.zeros((E, N), BF16)
    for h in range(HEADS):
        right = nt(pt[h], xin[h, 128:256, :])
        qc[h, 0:N, :] = jnp.where(low, right, 0.0).astype(BF16)
        qc[h, N : 2 * N, :] = jnp.where(low, 0.0, right).astype(BF16)
        cols = nt(xin[h], pt[h]).astype(BF16)
        xp[h] = cols
        rq[h, 0:E, :] = cols[128:192]
        rq[h, E:128, :] = zero
        rc[h, 0:E, :] = zero
        rc[h, E:128, :] = cols[192:256]

    def fill_bias(ref, at, rows, lanes, key_place, group):
        lq = level_of(lax.broadcasted_iota(jnp.int32, (rows, lanes), 1))
        mult = jnp.minimum(lq, level_of(key_place)) - (group - 1)
        value = jnp.where(mult > 0, jnp.log2(jnp.maximum(mult, 1).astype(F32)), NEG)
        ref[at : at + rows, :] = value

    wide = lax.broadcasted_iota(jnp.int32, (256, 256), 0)
    r256 = lax.broadcasted_iota(jnp.int32, (256, 128), 0)
    fill_bias(bias0, 0, 256, 256, wide, 0)

    def forward(score, values):
        peak = jnp.max(score, axis=0, keepdims=True)
        expo = jnp.exp2(score - peak)
        total = jnp.sum(expo, axis=0, keepdims=True)
        return peak, expo, total, nn(values, expo.astype(BF16))[E:128]

    local = [[] for _ in range(HEADS)]
    part1 = [None] * HEADS
    parts2 = [[] for _ in range(HEADS)]

    def local_forward(h):
        for t in range(2):
            qs = slice(256 * t, 256 * t + 256)
            score = nn(own[:, head_lanes(h)], rq[h, :, qs]) * SCALE2
            if t == 0:
                score = jnp.concatenate([score[0:256] + bias0[...], score[256:512]], axis=0)
            peak, expo, total, mix = forward(score, xp[h, 0:128, :])
            e0[h, :, qs] = expo
            num[h, :, qs] = mix
            local[h].append((peak, total))

    def remote_forward(h, a, b):
        ks = slice(256 + a, 256 + b)
        keys = rk[ks, head_lanes(h)]
        rkt[h, :, ks] = keys.T
        dp2[h, a:b, :] = nn(keys, rc[h, :, 0:128])
        score = nn(keys, rq[h, :, 0:128]) * SCALE2 + bias2[a:b, :]
        peak, expo, total, mix = forward(score, rkt[h, :, ks])
        e2[h, a:b, :] = expo
        at = 256 + 128 * len(parts2[h])
        nums[h, :, at : at + 128] = mix
        parts2[h].append((peak, total, at, a, b))

    local_forward(0)

    need("z32", "z48")
    rk[S6 : S6 + 16, :] = jnp.concatenate(
        [t32[...].astype(F32)[0:8], t48[...].astype(F32)[8:16]], axis=0
    ).astype(BF16)
    for e in (1, 2, 3, 4, 8, 12):
        move(f"p{e}", e, rk, S6, rk, S6 + 16 * e, 16)
    for b in (1, 2):
        need(f"ya{b}")
        for e in (4, 8, 12):
            move(f"x{e}_{b}", e, rk, Y_AT[b], rk, slot_at(e + b), X_ROWS[e])
    for e in (4, 12, 8):
        need(f"x{e}_0")
        move(f"x{e}_3", 3, rk, slot_at(e), rk, slot_at(e + 3), X_ROWS[e])
    move("yb1", 1, own, 64, rk, Y_AT[1] + 64, 192)
    move("yb3", 3, own, 64, rk, Y_AT[3] + 64, 64)
    move("yb2", 2, own, 64, rk, Y_AT[2] + 64, 64)

    def last_z(*slots):
        for d in slots:
            src = Y_AT[d] if d < 4 else slot_at(d)
            move(f"zl{d}", 16, rk, src, rk, S5 + 16 * d, 16)

    need("ya3")
    last_z(1, 2, 3, 4, 8, 12)

    local_forward(1)
    need("p1", "p2", "p3")
    for e in (4, 8, 12):
        move(f"pp{e}", e, rk, S6 + 16, rk, S6 + 16 * e + 16, 48)
    for e in (4, 12, 8):
        need(f"x{e}_1")
        last_z(e + 1)
    for e in (4, 12, 8):
        need(f"x{e}_2")
        last_z(e + 2)
    for e in (4, 12, 8):
        need(f"x{e}_3")
        last_z(e + 3)

    local_forward(2)
    fill_bias(bias2, 256, 256, 128, r256 & 63, 3)
    fill_bias(bias2, 512, 256, 128, r256 & 31, 4)
    fill_bias(bias2, 768, 256, 128, r256 & 15, 5)
    fill_bias(bias2, 1024, 256, 128, r256 & 7, 6)
    for h in range(HEADS):
        remote_forward(h, 256, 768)
    fill_bias(bias1, 0, 256, 256, wide, 1)
    fill_bias(bias2, 0, 256, 128, r256 & 127, 2)
    for h in range(HEADS):
        dp0[h] = nn(own[:, head_lanes(h)], rc[h])
    need("yb1", "yb2", "yb3")
    for h in range(HEADS):
        keys = rk[0:256, head_lanes(h)]
        rkt[h, :, 0:256] = keys.T
        dp1[h] = nn(keys, rc[h, :, 0:256])
        score = nn(keys, rq[h, :, 0:256]) * SCALE2 + bias1[...]
        peak, expo, total, mix = forward(score, rkt[h, :, 0:256])
        e1[h] = expo
        nums[h, :, 0:256] = mix
        part1[h] = (peak, total)
        remote_forward(h, 0, 256)
    for e in (4, 8, 12):
        need(f"p{e}", f"pp{e}")
    need(*(f"zl{d}" for d in range(16)))
    for h in range(HEADS):
        remote_forward(h, 768, 1280)

    def combine(h, lo, hi):
        t = lo // 256
        ls = slice(lo - 256 * t, hi - 256 * t)
        pieces = [(local[h][t][0][:, ls], local[h][t][1][:, ls], num[h, :, lo:hi])]
        if hi <= 256:
            pieces.append((part1[h][0][:, lo:hi], part1[h][1][:, lo:hi], nums[h, :, lo:hi]))
        if hi <= 128:
            for peak, total, at, _, _ in parts2[h]:
                pieces.append((peak, total, nums[h, :, at : at + 128]))
        top = pieces[0][0]
        for peak, _, _ in pieces[1:]:
            top = jnp.maximum(top, peak)
        factors = [jnp.exp2(peak - top) for peak, _, _ in pieces]
        inv = 1.0 / sum(f * total for f, (_, total, _) in zip(factors, pieces))
        gains = [f * inv for f in factors]
        attended = sum(g * mix for g, (_, _, mix) in zip(gains, pieces)).astype(BF16)
        cot = xp[h, 192:256, lo:hi].astype(F32)
        delta = jnp.sum(cot * attended.astype(F32), axis=0, keepdims=True)
        xp[h, 192:256, lo:hi] = attended
        return gains, delta

    def backward(h, dprob, expo, gain, delta, nq):
        probs = expo * gain
        dscore = (probs * (dprob - delta)).astype(BF16)
        both = jnp.concatenate([dscore, probs.astype(BF16)], axis=1)
        right = jnp.concatenate([qc[h, 0:nq, :], qc[h, N : N + nq, :]], axis=0)
        return dscore, nn(both, right)

    def remote_backward(h, which):
        _, _, _, a, b = parts2[h][which]
        gains, delta = first[h]
        dscore, dkv = backward(h, dp2[h, a:b, :], e2[h, a:b, :], gains[2 + which], delta, 128)
        return nn(rkt[h, :, 256 + a : 256 + b], dscore)[0:E], dkv

    first = [combine(h, 0, 128) for h in range(HEADS)]
    for h in range(HEADS):
        hs = head_lanes(h)
        dq, dkv = remote_backward(h, 0)
        gsend[512:1024, hs] = dkv.astype(BF16)
        xacc[0:64, hs] = dkv[0:64]
        xacc[64:96, hs] = dkv[256:288]
        xacc[96:128, hs] = dkv[384:416]
        dqz, dkv = remote_backward(h, 2)
        gsend[1024:1536, hs] = dkv.astype(BF16)
        pacc[0:64, hs] = dkv[0:64]
        pacc[64:128, hs] = dkv[256:320]
        dqa[h, :, 0:128] = dq + dqz
        dqa[h, :, 128:256] = jnp.zeros((E, 128), F32)
    r3_at = {4: 0, 8: 64, 12: 96}
    for e in (4, 8, 12):
        move(f"g{e}_3", 3, gsend, slot_at(e + 3), r3, r3_at[e], X_ROWS[e])
    z_at = {4: 0, 8: 64, 12: 128}
    x12_at = {4: 0, 8: 128, 12: 192}
    for e in (4, 8, 12):
        move(f"gp5{e}", e, gsend, S5 + 16 * e, rz5, z_at[e], 64)
        move(f"gp6{e}", e, gsend, S6 + 16 * e, rz6, z_at[e], 64)
    for e in (4, 8, 12):
        move(f"g{e}_12", e, gsend, slot_at(e + 1), rx12, x12_at[e], 2 * X_ROWS[e])

    second = [combine(h, 128, 256) for h in range(HEADS)]
    third = [combine(h, 256, 512) for h in range(HEADS)]
    delta_all = []
    for h in range(HEADS):
        hs = head_lanes(h)
        delta_all.append(jnp.concatenate([first[h][1], second[h][1], third[h][1]], axis=1))
        gain = jnp.concatenate([first[h][0][1], second[h][0][1]], axis=1)
        dscore, dkv = backward(h, dp1[h], e1[h], gain, delta_all[h][:, 0:256], 256)
        dqa[h, :, 0:256] += nn(rkt[h, :, 0:256], dscore)[0:E]
        yacc[0:64, hs] = dkv[0:64]
        gsend[64:256, hs] = dkv[64:256].astype(BF16)
        dq, dkv = remote_backward(h, 1)
        dqa[h, :, 0:128] += dq
        yacc[64:128, hs] = dkv[0:64]
        gsend[320:512, hs] = dkv[64:256].astype(BF16)
    move("gy3", 3, gsend, 384, ry, 384, 128)
    move("gy1", 1, gsend, 64, ry, 64, 192)
    move("gy2", 2, gsend, 320, ry, 320, 64)

    x0_at = {4: 0, 8: 64, 12: 96}
    for e in (4, 8, 12):
        n, at = X_ROWS[e], x0_at[e]
        need(f"g{e}_3")
        total = xacc[at : at + n, :] + r3[at : at + n, :].astype(F32)
        gsend[slot_at(e) : slot_at(e) + n, :] = total.astype(BF16)
        move(f"g{e}_0", e, gsend, slot_at(e), rx0, at, n)

    def local_backward(h):
        gain = jnp.concatenate([first[h][0][0], second[h][0][0], third[h][0][0]], axis=1)
        dscore, dkv = backward(h, dp0[h], e0[h], gain, delta_all[h], N)
        oacc[:, head_lanes(h)] = dkv
        dq = nn(xp[h, 0:128, :], dscore)[0:E]
        dq = jnp.concatenate([dq[:, 0:256] + dqa[h], dq[:, 256:512]], axis=1)
        done = nn(jnp.concatenate([xp[h, 192:256, :], dq.astype(BF16)], axis=0), pt[h])
        out[0, h] = done[0:E].astype(BF16)
        out[1, h] = (done[E:128] * 0.125).astype(BF16)

    local_backward(0)

    for e in (4, 8, 12):
        need(f"gp5{e}", f"gp6{e}")
    for b in (1, 2, 3):
        bs = slice(16 * b, 16 * b + 16)
        for part, got in ((0, rz5), (1, rz6)):
            total = pacc[64 * part + 16 * b : 64 * part + 16 * b + 16, :]
            for e in (4, 8, 12):
                total = total + got[z_at[e] + 16 * b : z_at[e] + 16 * b + 16, :].astype(F32)
            at = 32 * (b - 1) + 16 * part
            pz[at : at + 16, :] = total.astype(BF16)
        move(f"gpy{b}", b, pz, 32 * (b - 1), ryz, 32 * (b - 1), 32)
    for e in (4, 8, 12):
        need(f"g{e}_12")
    for b in (1, 2):
        part = yacc[64 * (b - 1) : 64 * b, :] + rx12[64 * (b - 1) : 64 * b, :].astype(F32)
        small = rx12[96 + 32 * b : 128 + 32 * b, :].astype(F32) + rx12[
            160 + 32 * b : 192 + 32 * b, :
        ].astype(F32)
        gsend[Y_AT[b] : Y_AT[b] + 32, :] = (part[0:32] + small).astype(BF16)
        gsend[Y_AT[b] + 32 : Y_AT[b] + 64, :] = part[32:64].astype(BF16)
        move(f"gya{b}", b, gsend, Y_AT[b], ry, Y_AT[b], 64)

    local_backward(1)

    need("gpy1", "gpy2", "gpy3")
    for part, got in ((0, rz5), (1, rz6)):
        total = pacc[64 * part : 64 * part + 16, :]
        for e in (4, 8, 12):
            total = total + got[z_at[e] : z_at[e] + 16, :].astype(F32)
        for b in (0, 1, 2):
            total = total + ryz[32 * b + 16 * part : 32 * b + 16 * part + 16, :].astype(F32)
        gsend[S5 + 256 * part : S5 + 256 * part + 16, :] = total.astype(BF16)
    move("gz16", 16, gsend, S5, rzz, 0, 16)
    move("gz32", 32, gsend, S6, rzz, 16, 16)
    move("gz48", 48, gsend, S6, rzz, 32, 16)

    local_backward(2)

    stores = [pltpu.make_async_copy(out.at[0:2], out_hbm.at[0:2], out_sem.at[0])]
    stores[0].start()

    need("gy1", "gy2", "gy3")
    for h in range(HEADS):
        hs = head_lanes(h)
        b256 = oacc[128:256, hs] + ry[128:256, hs].astype(F32)
        whole = jnp.concatenate([b256, oacc[256:512, hs]], axis=0)
        early[h] = nn(whole.T.astype(BF16), pt[h, 128:512, :])
        b128 = oacc[64:128, hs]
        for b in (1, 2, 3):
            b128 = b128 + ry[Y_AT[b] + 64 : Y_AT[b] + 128, hs].astype(F32)
        oacc[64:128, hs] = b128

    need("g4_0", "g8_0", "g12_0", "gya1", "gya2", "gz16", "gz32", "gz48")
    for h in range(HEADS):
        hs = head_lanes(h)
        a = oacc[0:64, hs] + rx0[0:64, hs].astype(F32)
        for b in (1, 2, 3):
            a = a + ry[Y_AT[b] : Y_AT[b] + 64, hs].astype(F32)
        a32 = a[0:32] + rx0[64:96, hs].astype(F32) + rx0[96:128, hs].astype(F32)
        a16 = a32[0:16] + rzz[0:16, hs].astype(F32)
        a8 = a16[0:8] + rzz[16:32, hs].astype(F32)[0:8] + rzz[32:48, hs].astype(F32)[8:16]
        whole = jnp.concatenate([a8, a16[8:16], a32[16:32], a[32:64], oacc[64:128, hs]], axis=0)
        done = early[h] + nn(whole.T.astype(BF16), pt[h, 0:128, :])
        out[2, h] = (done[0:E] * 0.125).astype(BF16)
        out[3, h] = done[E:128].astype(BF16)
    stores.append(pltpu.make_async_copy(out.at[2:4], out_hbm.at[2:4], out_sem.at[1]))
    stores[1].start()
    for copy in copies.values():
        copy.wait_send()
    for store in stores:
        store.wait()


def hand_out(res, o_hbm, gq_hbm, gk_hbm, gv_hbm, held, in_sem, out_sem):
    outs = (o_hbm, gq_hbm, gk_hbm, gv_hbm)
    loads = [pltpu.make_async_copy(res.at[i], held.at[i], in_sem.at[i]) for i in range(4)]
    stores = [pltpu.make_async_copy(held.at[i], outs[i], out_sem.at[i]) for i in range(4)]
    for load in loads:
        load.start()
    for load, store in zip(loads, stores):
        load.wait()
        store.start()
    for store in stores:
        store.wait()


COPIES = 72


def per_device(tile_query, tile_key, tile_value, out_cotangent):
    shape = (HEADS, E, N)
    args = [a.reshape(shape) for a in (tile_query, tile_key, tile_value, out_cotangent)]
    vm = pltpu.VMEM
    anywhere = pl.BlockSpec(memory_space=pl.ANY)
    res = pl.pallas_call(
        body,
        out_shape=jax.ShapeDtypeStruct((4, *shape), BF16),
        in_specs=[anywhere] * 4,
        out_specs=anywhere,
        scratch_shapes=[
            vm((4, *shape), BF16),
            vm((HEADS, 256, N), BF16),
            vm((HEADS, N, N), BF16),
            vm((N, W), BF16),
            vm((16, W), BF16),
            vm((HEADS, 2 * N, 128), BF16),
            vm((HEADS, 256, N), BF16),
            vm((HEADS, 128, N), BF16),
            vm((HEADS, 128, N), BF16),
            vm((256, 256), F32),
            vm((256, 256), F32),
            vm((1280, 128), F32),
            vm((HEADS, N, N), F32),
            vm((HEADS, N, N), F32),
            vm((HEADS, 256, 256), F32),
            vm((HEADS, 256, 256), F32),
            vm((HEADS, 1280, 128), F32),
            vm((HEADS, 1280, 128), F32),
            vm((HEADS, E, N), F32),
            vm((HEADS, E, 640), F32),
            vm((HEADS, E, 256), F32),
            vm((HEADS, 128, N), F32),
            vm((ROWS, W), BF16),
            vm((HEADS, 128, ROWS), BF16),
            vm((16, W), BF16),
            vm((16, W), BF16),
            vm((ROWS, W), BF16),
            vm((128, W), F32),
            vm((128, W), F32),
            vm((128, W), F32),
            vm((N, W), F32),
            vm((128, W), BF16),
            vm((256, W), BF16),
            vm((128, W), BF16),
            vm((192, W), BF16),
            vm((192, W), BF16),
            vm((512, W), BF16),
            vm((96, W), BF16),
            vm((96, W), BF16),
            vm((48, W), BF16),
            pltpu.SemaphoreType.DMA((4,)),
            pltpu.SemaphoreType.DMA((2,)),
            pltpu.SemaphoreType.DMA((COPIES,)),
            pltpu.SemaphoreType.DMA((COPIES,)),
        ],
        compiler_params=pltpu.CompilerParams(
            collective_id=0, has_side_effects=True, vmem_limit_bytes=62 * 2**20
        ),
        name="dilated",
    )(*args)
    outs = pl.pallas_call(
        hand_out,
        out_shape=[jax.ShapeDtypeStruct((HEADS * E, N), BF16)] * 4,
        in_specs=[anywhere],
        out_specs=[anywhere] * 4,
        scratch_shapes=[
            vm((4, HEADS * E, N), BF16),
            pltpu.SemaphoreType.DMA((4,)),
            pltpu.SemaphoreType.DMA((4,)),
        ],
        compiler_params=pltpu.CompilerParams(vmem_limit_bytes=62 * 2**20),
        name="outputs",
    )(res.reshape(4, HEADS * E, N))
    return tuple(outs)


def solution(mesh):
    spec = P("head", "seq")
    return jax.shard_map(
        per_device, mesh=mesh, in_specs=(spec,) * 4, out_specs=(spec,) * 4, check_vma=False
    )
```

```python
import math

import jax
import jax.numpy as jnp
from jax import lax
from jax.experimental import pallas as pl
from jax.experimental.pallas import tpu as pltpu
from jax.sharding import PartitionSpec as P

E = 64
HEADS = 3
N = 512
W = HEADS * 128
F32 = jnp.float32
BF16 = jnp.bfloat16
NEG = -1e30
SCALE2 = math.log2(math.e) / math.sqrt(E)

ROWS = 1536
Y_AT, Y_ROWS = {1: 0, 2: 256, 3: 384}, {1: 256, 2: 128, 3: 128}
X_AT, X_ROWS = {4: 512, 8: 768, 12: 896}, {4: 64, 8: 32, 12: 32}
S5, S6 = 1024, 1280


def slot_at(d):
    return X_AT[d // 4 * 4] + X_ROWS[d // 4 * 4] * (d % 4)


def nn(a, b):
    return lax.dot_general(a, b, (((1,), (0,)), ((), ())), preferred_element_type=F32)


def nt(a, b):
    return lax.dot_general(a, b, (((1,), (1,)), ((), ())), preferred_element_type=F32)


def level_of(index):
    level = jnp.zeros(index.shape, jnp.int32)
    for bound in (8, 16, 32, 64, 128, 256):
        level = level + (index < bound).astype(jnp.int32)
    return level


def body(
    q_hbm, k_hbm, v_hbm, c_hbm, out,
    xin, pt, own, d6, qc, xp, rq, rc, bias0, bias1, bias2,
    e0, dp0, e1, dp1, e2, dp2, num, nums, dqa, early,
    rk, rkt, t32, t48, gsend, yacc, xacc, pacc, oacc,
    rx0, rx12, r3, rz5, rz6, ry, pz, ryz, rzz,
    in_sem, send_sem, recv_sem,
):
    me = lax.axis_index("seq")
    head0 = lax.axis_index("head") * HEADS
    z, x, y = lax.div(me, 16), lax.rem(lax.div(me, 4), 4), lax.rem(me, 4)

    def flipped(v, bits):
        if bits == 0:
            return v
        if bits == 1:
            return v + 1 - 2 * lax.rem(v, 2)
        if bits == 2:
            return lax.rem(v + 2, 4)
        return 3 - v

    peer = {e: flipped(z, e // 16) * 16 + flipped(x, e // 4 % 4) * 4 + flipped(y, e % 4)
            for e in (1, 2, 3, 4, 8, 12, 16, 32, 48)}

    loads = []
    for at, src in enumerate((k_hbm, v_hbm, q_hbm, c_hbm)):
        load = pltpu.make_async_copy(src, xin.at[:, pl.ds(64 * at, 64), :], in_sem.at[at])
        load.start()
        loads.append(load)
    barrier = pltpu.get_barrier_semaphore()
    for e in peer:
        pl.semaphore_signal(
            barrier, inc=1, device_id={"seq": peer[e]}, device_id_type=pl.DeviceIdType.MESH
        )

    copies, landed = {}, set()

    def send(key, src, dst, e):
        at = len(copies)
        copies[key] = pltpu.make_async_remote_copy(
            src_ref=src,
            dst_ref=dst,
            send_sem=send_sem.at[at],
            recv_sem=recv_sem.at[at],
            device_id={"seq": peer[e]},
            device_id_type=pl.DeviceIdType.MESH,
        )
        copies[key].start()

    def need(*keys):
        for key in keys:
            if key not in landed:
                copies[key].wait_recv()
                landed.add(key)

    def move(key, e, src, a, dst, b, n):
        send(key, src.at[a : a + n], dst.at[b : b + n], e)

    def head_lanes(h):
        return slice(128 * h, 128 * h + 128)

    place = lax.broadcasted_iota(jnp.int32, (N, 128), 0)
    lane = lax.broadcasted_iota(jnp.int32, (8, 128), 1)
    u = 64 * place
    for bits in range(4, 10):
        u = jnp.where(place >= 1 << (bits - 1), ((2 * place + 1) << (9 - bits)) & (N - 1), u)
    for h in range(HEADS):
        for t in range(4):
            tile = (lane + (128 * t + N) - (head0 + h)) & (N - 1)
            hot = u == jnp.broadcast_to(tile[0:1], (N, 128))
            pt[h, :, 128 * t : 128 * t + 128] = jnp.where(hot, 1.0, 0.0).astype(BF16)

    for load in loads[0:2]:
        load.wait()
    for h in range(HEADS):
        rows = nt(pt[h], xin[h, 0:128, :])
        own[:, head_lanes(h)] = rows.astype(BF16)
        d6[:, head_lanes(h)] = jnp.concatenate([rows[0:8]] * 2, axis=0).astype(BF16)

    pl.semaphore_wait(barrier, len(peer))
    move("x4_0", 4, own, 0, rk, slot_at(4), 64)
    move("ya1", 1, own, 0, rk, Y_AT[1], 64)
    send("z32", d6, t32, 32)
    send("z48", d6, t48, 48)
    move("ya3", 3, own, 0, rk, Y_AT[3], 64)
    move("x8_0", 8, own, 0, rk, slot_at(8), 32)
    move("ya2", 2, own, 0, rk, Y_AT[2], 64)
    move("x12_0", 12, own, 0, rk, slot_at(12), 32)
    move("zl0", 16, own, 0, rk, S5, 16)

    for load in loads[2:4]:
        load.wait()
    low = lax.broadcasted_iota(jnp.int32, (N, 128), 1) < E
    zero = jnp.zeros((E, N), BF16)
    for h in range(HEADS):
        right = nt(pt[h], xin[h, 128:256, :])
        qc[h, 0:N, :] = jnp.where(low, right, 0.0).astype(BF16)
        qc[h, N : 2 * N, :] = jnp.where(low, 0.0, right).astype(BF16)
        cols = nt(xin[h], pt[h]).astype(BF16)
        xp[h] = cols
        rq[h, 0:E, :] = cols[128:192]
        rq[h, E:128, :] = zero
        rc[h, 0:E, :] = zero
        rc[h, E:128, :] = cols[192:256]

    def fill_bias(ref, at, rows, lanes, key_place, group):
        lq = level_of(lax.broadcasted_iota(jnp.int32, (rows, lanes), 1))
        mult = jnp.minimum(lq, level_of(key_place)) - (group - 1)
        value = jnp.where(mult > 0, jnp.log2(jnp.maximum(mult, 1).astype(F32)), NEG)
        ref[at : at + rows, :] = value

    wide = lax.broadcasted_iota(jnp.int32, (256, 256), 0)
    r256 = lax.broadcasted_iota(jnp.int32, (256, 128), 0)
    fill_bias(bias0, 0, 256, 256, wide, 0)

    def forward(score, values):
        peak = jnp.max(score, axis=0, keepdims=True)
        expo = jnp.exp2(score - peak)
        total = jnp.sum(expo, axis=0, keepdims=True)
        return peak, expo, total, nn(values, expo.astype(BF16))[E:128]

    local = [[] for _ in range(HEADS)]
    part1 = [None] * HEADS
    parts2 = [[] for _ in range(HEADS)]

    def local_forward(h):
        for t in range(2):
            qs = slice(256 * t, 256 * t + 256)
            score = nn(own[:, head_lanes(h)], rq[h, :, qs]) * SCALE2
            if t == 0:
                score = jnp.concatenate([score[0:256] + bias0[...], score[256:512]], axis=0)
            peak, expo, total, mix = forward(score, xp[h, 0:128, :])
            e0[h, :, qs] = expo
            num[h, :, qs] = mix
            local[h].append((peak, total))

    def remote_forward(h, a, b):
        ks = slice(256 + a, 256 + b)
        keys = rk[ks, head_lanes(h)]
        rkt[h, :, ks] = keys.T
        dp2[h, a:b, :] = nn(keys, rc[h, :, 0:128])
        score = nn(keys, rq[h, :, 0:128]) * SCALE2 + bias2[a:b, :]
        peak, expo, total, mix = forward(score, rkt[h, :, ks])
        e2[h, a:b, :] = expo
        at = 256 + 128 * len(parts2[h])
        nums[h, :, at : at + 128] = mix
        parts2[h].append((peak, total, at, a, b))

    local_forward(0)

    need("z32", "z48")
    rk[S6 : S6 + 16, :] = jnp.concatenate(
        [t32[...].astype(F32)[0:8], t48[...].astype(F32)[8:16]], axis=0
    ).astype(BF16)
    for e in (1, 2, 3, 4, 8, 12):
        move(f"p{e}", e, rk, S6, rk, S6 + 16 * e, 16)
    for b in (1, 2):
        need(f"ya{b}")
        for e in (4, 8, 12):
            move(f"x{e}_{b}", e, rk, Y_AT[b], rk, slot_at(e + b), X_ROWS[e])
    for e in (4, 12, 8):
        need(f"x{e}_0")
        move(f"x{e}_3", 3, rk, slot_at(e), rk, slot_at(e + 3), X_ROWS[e])
    move("yb1", 1, own, 64, rk, Y_AT[1] + 64, 192)
    move("yb3", 3, own, 64, rk, Y_AT[3] + 64, 64)
    move("yb2", 2, own, 64, rk, Y_AT[2] + 64, 64)

    def last_z(*slots):
        for d in slots:
            src = Y_AT[d] if d < 4 else slot_at(d)
            move(f"zl{d}", 16, rk, src, rk, S5 + 16 * d, 16)

    need("ya3")
    last_z(1, 2, 3, 4, 8, 12)

    local_forward(1)
    need("p1", "p2", "p3")
    for e in (4, 8, 12):
        move(f"pp{e}", e, rk, S6 + 16, rk, S6 + 16 * e + 16, 48)
    for e in (4, 12, 8):
        need(f"x{e}_1")
        last_z(e + 1)
    for e in (4, 12, 8):
        need(f"x{e}_2")
        last_z(e + 2)
    for e in (4, 12, 8):
        need(f"x{e}_3")
        last_z(e + 3)

    local_forward(2)
    fill_bias(bias2, 256, 256, 128, r256 & 63, 3)
    fill_bias(bias2, 512, 256, 128, r256 & 31, 4)
    fill_bias(bias2, 768, 256, 128, r256 & 15, 5)
    fill_bias(bias2, 1024, 256, 128, r256 & 7, 6)
    for h in range(HEADS):
        remote_forward(h, 256, 768)
    fill_bias(bias1, 0, 256, 256, wide, 1)
    fill_bias(bias2, 0, 256, 128, r256 & 127, 2)
    for h in range(HEADS):
        dp0[h] = nn(own[:, head_lanes(h)], rc[h])
    need("yb1", "yb2", "yb3")
    for h in range(HEADS):
        keys = rk[0:256, head_lanes(h)]
        rkt[h, :, 0:256] = keys.T
        dp1[h] = nn(keys, rc[h, :, 0:256])
        score = nn(keys, rq[h, :, 0:256]) * SCALE2 + bias1[...]
        peak, expo, total, mix = forward(score, rkt[h, :, 0:256])
        e1[h] = expo
        nums[h, :, 0:256] = mix
        part1[h] = (peak, total)
        remote_forward(h, 0, 256)
    for e in (4, 8, 12):
        need(f"p{e}", f"pp{e}")
    for h in range(HEADS):
        remote_forward(h, 1024, 1280)
    need(*(f"zl{d}" for d in range(16)))
    for h in range(HEADS):
        remote_forward(h, 768, 1024)

    def combine(h, lo, hi):
        t = lo // 256
        ls = slice(lo - 256 * t, hi - 256 * t)
        pieces = [(local[h][t][0][:, ls], local[h][t][1][:, ls], num[h, :, lo:hi])]
        if hi <= 256:
            pieces.append((part1[h][0][:, lo:hi], part1[h][1][:, lo:hi], nums[h, :, lo:hi]))
        if hi <= 128:
            for peak, total, at, _, _ in parts2[h]:
                pieces.append((peak, total, nums[h, :, at : at + 128]))
        top = pieces[0][0]
        for peak, _, _ in pieces[1:]:
            top = jnp.maximum(top, peak)
        factors = [jnp.exp2(peak - top) for peak, _, _ in pieces]
        inv = 1.0 / sum(f * total for f, (_, total, _) in zip(factors, pieces))
        gains = [f * inv for f in factors]
        attended = sum(g * mix for g, (_, _, mix) in zip(gains, pieces)).astype(BF16)
        cot = xp[h, 192:256, lo:hi].astype(F32)
        delta = jnp.sum(cot * attended.astype(F32), axis=0, keepdims=True)
        xp[h, 192:256, lo:hi] = attended
        return gains, delta

    def backward(h, dprob, expo, gain, delta, nq):
        probs = expo * gain
        dscore = (probs * (dprob - delta)).astype(BF16)
        both = jnp.concatenate([dscore, probs.astype(BF16)], axis=1)
        right = jnp.concatenate([qc[h, 0:nq, :], qc[h, N : N + nq, :]], axis=0)
        return dscore, nn(both, right)

    def remote_backward(h, which):
        _, _, _, a, b = parts2[h][which]
        gains, delta = first[h]
        dscore, dkv = backward(h, dp2[h, a:b, :], e2[h, a:b, :], gains[2 + which], delta, 128)
        return dkv, dscore, rkt[h, :, 256 + a : 256 + b]

    first = [combine(h, 0, 128) for h in range(HEADS)]
    z_at = {4: 0, 8: 64, 12: 128}
    queries = [[] for _ in range(HEADS)]
    for h in range(HEADS):
        hs = head_lanes(h)
        for which, at, kept in ((3, S5, 0), (2, S6, 64)):
            dkv, *rest = remote_backward(h, which)
            queries[h].append(rest)
            gsend[at : at + 256, hs] = dkv.astype(BF16)
            pacc[kept : kept + 64, hs] = dkv[0:64]
    for e in (4, 8, 12):
        move(f"gp5{e}", e, gsend, S5 + 16 * e, rz5, z_at[e], 64)
        move(f"gp6{e}", e, gsend, S6 + 16 * e, rz6, z_at[e], 64)
    r3_at = {4: 0, 8: 64, 12: 96}
    x12_at = {4: 0, 8: 128, 12: 192}
    for h in range(HEADS):
        hs = head_lanes(h)
        dkv, *rest = remote_backward(h, 0)
        queries[h].append(rest)
        gsend[512:1024, hs] = dkv.astype(BF16)
        xacc[0:64, hs] = dkv[0:64]
        xacc[64:96, hs] = dkv[256:288]
        xacc[96:128, hs] = dkv[384:416]
    for e in (4, 8, 12):
        move(f"g{e}_3", 3, gsend, slot_at(e + 3), r3, r3_at[e], X_ROWS[e])
    for e in (4, 8, 12):
        move(f"g{e}_12", e, gsend, slot_at(e + 1), rx12, x12_at[e], 2 * X_ROWS[e])

    second = [combine(h, 128, 256) for h in range(HEADS)]
    third = [combine(h, 256, 512) for h in range(HEADS)]
    delta_all = []
    for h in range(HEADS):
        hs = head_lanes(h)
        delta_all.append(jnp.concatenate([first[h][1], second[h][1], third[h][1]], axis=1))
        gain = jnp.concatenate([first[h][0][1], second[h][0][1]], axis=1)
        dscore, dkv = backward(h, dp1[h], e1[h], gain, delta_all[h][:, 0:256], 256)
        dqa[h] = nn(rkt[h, :, 0:256], dscore)[0:E]
        yacc[0:64, hs] = dkv[0:64]
        gsend[64:256, hs] = dkv[64:256].astype(BF16)
        dkv, *rest = remote_backward(h, 1)
        dqa[h, :, 0:128] += sum(nn(values, ds)[0:E] for ds, values in [*queries[h], rest])
        yacc[64:128, hs] = dkv[0:64]
        gsend[320:512, hs] = dkv[64:256].astype(BF16)
    move("gy3", 3, gsend, 384, ry, 384, 128)
    move("gy1", 1, gsend, 64, ry, 64, 192)
    move("gy2", 2, gsend, 320, ry, 320, 64)

    x0_at = {4: 0, 8: 64, 12: 96}
    for e in (4, 8, 12):
        n, at = X_ROWS[e], x0_at[e]
        need(f"g{e}_3")
        total = xacc[at : at + n, :] + r3[at : at + n, :].astype(F32)
        gsend[slot_at(e) : slot_at(e) + n, :] = total.astype(BF16)
        move(f"g{e}_0", e, gsend, slot_at(e), rx0, at, n)

    def local_backward(h):
        gain = jnp.concatenate([first[h][0][0], second[h][0][0], third[h][0][0]], axis=1)
        dscore, dkv = backward(h, dp0[h], e0[h], gain, delta_all[h], N)
        oacc[:, head_lanes(h)] = dkv
        dq = nn(xp[h, 0:128, :], dscore)[0:E]
        dq = jnp.concatenate([dq[:, 0:256] + dqa[h], dq[:, 256:512]], axis=1)
        done = nn(jnp.concatenate([xp[h, 192:256, :], dq.astype(BF16)], axis=0), pt[h])
        out[0, h] = done[0:E].astype(BF16)
        out[1, h] = (done[E:128] * 0.125).astype(BF16)

    local_backward(0)

    for e in (4, 8, 12):
        need(f"gp5{e}", f"gp6{e}")
    for b in (1, 2, 3):
        bs = slice(16 * b, 16 * b + 16)
        for part, got in ((0, rz5), (1, rz6)):
            total = pacc[64 * part + 16 * b : 64 * part + 16 * b + 16, :]
            for e in (4, 8, 12):
                total = total + got[z_at[e] + 16 * b : z_at[e] + 16 * b + 16, :].astype(F32)
            at = 32 * (b - 1) + 16 * part
            pz[at : at + 16, :] = total.astype(BF16)
        move(f"gpy{b}", b, pz, 32 * (b - 1), ryz, 32 * (b - 1), 32)
    for e in (4, 8, 12):
        need(f"g{e}_12")
    for b in (1, 2):
        part = yacc[64 * (b - 1) : 64 * b, :] + rx12[64 * (b - 1) : 64 * b, :].astype(F32)
        small = rx12[96 + 32 * b : 128 + 32 * b, :].astype(F32) + rx12[
            160 + 32 * b : 192 + 32 * b, :
        ].astype(F32)
        gsend[Y_AT[b] : Y_AT[b] + 32, :] = (part[0:32] + small).astype(BF16)
        gsend[Y_AT[b] + 32 : Y_AT[b] + 64, :] = part[32:64].astype(BF16)
        move(f"gya{b}", b, gsend, Y_AT[b], ry, Y_AT[b], 64)

    local_backward(1)

    need("gpy1", "gpy2", "gpy3")
    for part, got in ((0, rz5), (1, rz6)):
        total = pacc[64 * part : 64 * part + 16, :]
        for e in (4, 8, 12):
            total = total + got[z_at[e] : z_at[e] + 16, :].astype(F32)
        for b in (0, 1, 2):
            total = total + ryz[32 * b + 16 * part : 32 * b + 16 * part + 16, :].astype(F32)
        gsend[S5 + 256 * part : S5 + 256 * part + 16, :] = total.astype(BF16)
    move("gz16", 16, gsend, S5, rzz, 0, 16)
    move("gz32", 32, gsend, S6, rzz, 16, 16)
    move("gz48", 48, gsend, S6, rzz, 32, 16)

    local_backward(2)

    need("gy1", "gy2", "gy3")
    for h in range(HEADS):
        hs = head_lanes(h)
        b256 = oacc[128:256, hs] + ry[128:256, hs].astype(F32)
        whole = jnp.concatenate([b256, oacc[256:512, hs]], axis=0)
        early[h] = nn(whole.T.astype(BF16), pt[h, 128:512, :])
        b128 = oacc[64:128, hs]
        for b in (1, 2, 3):
            b128 = b128 + ry[Y_AT[b] + 64 : Y_AT[b] + 128, hs].astype(F32)
        oacc[64:128, hs] = b128

    need("g4_0", "g8_0", "g12_0", "gya1", "gya2", "gz16", "gz32", "gz48")
    for h in range(HEADS):
        hs = head_lanes(h)
        a = oacc[0:64, hs] + rx0[0:64, hs].astype(F32)
        for b in (1, 2, 3):
            a = a + ry[Y_AT[b] : Y_AT[b] + 64, hs].astype(F32)
        a32 = a[0:32] + rx0[64:96, hs].astype(F32) + rx0[96:128, hs].astype(F32)
        a16 = a32[0:16] + rzz[0:16, hs].astype(F32)
        a8 = a16[0:8] + rzz[16:32, hs].astype(F32)[0:8] + rzz[32:48, hs].astype(F32)[8:16]
        whole = jnp.concatenate([a8, a16[8:16], a32[16:32], a[32:64], oacc[64:128, hs]], axis=0)
        done = early[h] + nn(whole.T.astype(BF16), pt[h, 0:128, :])
        out[2, h] = (done[0:E] * 0.125).astype(BF16)
        out[3, h] = done[E:128].astype(BF16)
    for copy in copies.values():
        copy.wait_send()


def hand_out(res, o_hbm, gq_hbm, gk_hbm, gv_hbm, sem):
    stores = [
        pltpu.make_async_copy(res.at[at], dst, sem.at[at])
        for at, dst in enumerate((o_hbm, gq_hbm, gk_hbm, gv_hbm))
    ]
    for store in stores:
        store.start()
    for store in stores:
        store.wait()


COPIES = 72


def per_device(tile_query, tile_key, tile_value, out_cotangent):
    shape = (HEADS, E, N)
    args = [
        pltpu.with_memory_space_constraint(a.reshape(shape), pltpu.HBM)
        for a in (tile_query, tile_key, tile_value, out_cotangent)
    ]
    vm = pltpu.VMEM
    anywhere = pl.BlockSpec(memory_space=pl.ANY)
    res = pl.pallas_call(
        body,
        out_shape=jax.ShapeDtypeStruct((4, *shape), BF16),
        in_specs=[anywhere] * 4,
        out_specs=pl.BlockSpec(memory_space=pltpu.VMEM),
        scratch_shapes=[
            vm((HEADS, 256, N), BF16),
            vm((HEADS, N, N), BF16),
            vm((N, W), BF16),
            vm((16, W), BF16),
            vm((HEADS, 2 * N, 128), BF16),
            vm((HEADS, 256, N), BF16),
            vm((HEADS, 128, N), BF16),
            vm((HEADS, 128, N), BF16),
            vm((256, 256), F32),
            vm((256, 256), F32),
            vm((1280, 128), F32),
            vm((HEADS, N, N), F32),
            vm((HEADS, N, N), F32),
            vm((HEADS, 256, 256), F32),
            vm((HEADS, 256, 256), F32),
            vm((HEADS, 1280, 128), F32),
            vm((HEADS, 1280, 128), F32),
            vm((HEADS, E, N), F32),
            vm((HEADS, E, 768), F32),
            vm((HEADS, E, 256), F32),
            vm((HEADS, 128, N), F32),
            vm((ROWS, W), BF16),
            vm((HEADS, 128, ROWS), BF16),
            vm((16, W), BF16),
            vm((16, W), BF16),
            vm((ROWS, W), BF16),
            vm((128, W), F32),
            vm((128, W), F32),
            vm((128, W), F32),
            vm((N, W), F32),
            vm((128, W), BF16),
            vm((256, W), BF16),
            vm((128, W), BF16),
            vm((192, W), BF16),
            vm((192, W), BF16),
            vm((512, W), BF16),
            vm((96, W), BF16),
            vm((96, W), BF16),
            vm((48, W), BF16),
            pltpu.SemaphoreType.DMA((4,)),
            pltpu.SemaphoreType.DMA((COPIES,)),
            pltpu.SemaphoreType.DMA((COPIES,)),
        ],
        compiler_params=pltpu.CompilerParams(
            collective_id=0, has_side_effects=True, vmem_limit_bytes=44 * 2**20
        ),
        name="dilated",
    )(*args)
    outs = pl.pallas_call(
        hand_out,
        out_shape=[jax.ShapeDtypeStruct((HEADS * E, N), BF16)] * 4,
        in_specs=[anywhere],
        out_specs=[anywhere] * 4,
        scratch_shapes=[
            pltpu.SemaphoreType.DMA((4,)),
        ],
        compiler_params=pltpu.CompilerParams(vmem_limit_bytes=2**20),
        name="outputs",
    )(res.reshape(4, HEADS * E, N))
    return tuple(outs)


def solution(mesh):
    spec = P("head", "seq")
    return jax.shard_map(
        per_device, mesh=mesh, in_specs=(spec,) * 4, out_specs=(spec,) * 4, check_vma=False
    )
```

```python
import math

import jax
import jax.numpy as jnp
from jax import lax
from jax.experimental import pallas as pl
from jax.experimental.pallas import tpu as pltpu
from jax.sharding import PartitionSpec as P

E = 64
HEADS = 3
N = 512
W = HEADS * 128
F32 = jnp.float32
BF16 = jnp.bfloat16
NEG = -1e30
SCALE2 = math.log2(math.e) / math.sqrt(E)

ROWS = 1536
Y_AT, Y_ROWS = {1: 0, 2: 256, 3: 384}, {1: 256, 2: 128, 3: 128}
X_AT, X_ROWS = {4: 512, 8: 768, 12: 896}, {4: 64, 8: 32, 12: 32}
S5, S6 = 1024, 1280


def slot_at(d):
    return X_AT[d // 4 * 4] + X_ROWS[d // 4 * 4] * (d % 4)


def nn(a, b):
    return lax.dot_general(a, b, (((1,), (0,)), ((), ())), preferred_element_type=F32)


def nt(a, b):
    return lax.dot_general(a, b, (((1,), (1,)), ((), ())), preferred_element_type=F32)


def level_of(index):
    level = jnp.zeros(index.shape, jnp.int32)
    for bound in (8, 16, 32, 64, 128, 256):
        level = level + (index < bound).astype(jnp.int32)
    return level


def body(
    q_hbm, k_hbm, v_hbm, c_hbm, out,
    xin, pt, own, d6, qc, xp, rq, rc, bias0, bias1, bias2,
    e0, e1, e2, dp2, num, nums, dqa, early,
    rk, rkt, t32, t48, gsend, yacc, xacc, pacc, oacc,
    rx0, rx12, r3, rz5, rz6, ry, pz, ryz, rzz,
    in_sem, send_sem, recv_sem,
):
    me = lax.axis_index("seq")
    head0 = lax.axis_index("head") * HEADS
    z, x, y = lax.div(me, 16), lax.rem(lax.div(me, 4), 4), lax.rem(me, 4)

    def flipped(v, bits):
        if bits == 0:
            return v
        if bits == 1:
            return v + 1 - 2 * lax.rem(v, 2)
        if bits == 2:
            return lax.rem(v + 2, 4)
        return 3 - v

    peer = {e: flipped(z, e // 16) * 16 + flipped(x, e // 4 % 4) * 4 + flipped(y, e % 4)
            for e in (1, 2, 3, 4, 8, 12, 16, 32, 48)}

    loads = []
    for at, src in enumerate((k_hbm, v_hbm, q_hbm, c_hbm)):
        load = pltpu.make_async_copy(src, xin.at[:, pl.ds(64 * at, 64), :], in_sem.at[at])
        load.start()
        loads.append(load)
    barrier = pltpu.get_barrier_semaphore()
    for e in peer:
        pl.semaphore_signal(
            barrier, inc=1, device_id={"seq": peer[e]}, device_id_type=pl.DeviceIdType.MESH
        )

    copies, landed = {}, set()

    def send(key, src, dst, e):
        at = len(copies)
        copies[key] = pltpu.make_async_remote_copy(
            src_ref=src,
            dst_ref=dst,
            send_sem=send_sem.at[at],
            recv_sem=recv_sem.at[at],
            device_id={"seq": peer[e]},
            device_id_type=pl.DeviceIdType.MESH,
        )
        copies[key].start()

    def need(*keys):
        for key in keys:
            if key not in landed:
                copies[key].wait_recv()
                landed.add(key)

    def move(key, e, src, a, dst, b, n):
        send(key, src.at[a : a + n], dst.at[b : b + n], e)

    def head_lanes(h):
        return slice(128 * h, 128 * h + 128)

    def one_hot(lo, hi):
        place = lax.broadcasted_iota(jnp.int32, (hi - lo, 128), 0) + lo
        lane = lax.broadcasted_iota(jnp.int32, (8, 128), 1)
        u = 64 * place
        for bits in range(4, hi.bit_length()):
            u = jnp.where(place >= 1 << (bits - 1), ((2 * place + 1) << (9 - bits)) & (N - 1), u)
        for h in range(HEADS):
            for t in range(4):
                tile = (lane + (128 * t + N) - (head0 + h)) & (N - 1)
                hot = u == jnp.broadcast_to(tile[0:1], (hi - lo, 128))
                pt[h, lo:hi, 128 * t : 128 * t + 128] = jnp.where(hot, 1.0, 0.0).astype(BF16)

    one_hot(0, 64)
    for load in loads[0:2]:
        load.wait()
    for h in range(HEADS):
        rows = nt(pt[h, 0:64, :], xin[h, 0:128, :])
        own[0:64, head_lanes(h)] = rows.astype(BF16)
        d6[:, head_lanes(h)] = jnp.concatenate([rows[0:8]] * 2, axis=0).astype(BF16)

    pl.semaphore_wait(barrier, len(peer))
    move("x4_0", 4, own, 0, rk, slot_at(4), 64)
    move("ya1", 1, own, 0, rk, Y_AT[1], 64)
    send("z32", d6, t32, 32)
    send("z48", d6, t48, 48)
    move("ya3", 3, own, 0, rk, Y_AT[3], 64)
    move("x8_0", 8, own, 0, rk, slot_at(8), 32)
    move("ya2", 2, own, 0, rk, Y_AT[2], 64)
    move("x12_0", 12, own, 0, rk, slot_at(12), 32)
    move("zl0", 16, own, 0, rk, S5, 16)

    one_hot(64, N)
    for load in loads[2:4]:
        load.wait()
    low = lax.broadcasted_iota(jnp.int32, (N, 128), 1) < E
    zero = jnp.zeros((E, N), BF16)
    for h in range(HEADS):
        own[64:N, head_lanes(h)] = nt(pt[h, 64:N, :], xin[h, 0:128, :]).astype(BF16)
        right = nt(pt[h], xin[h, 128:256, :])
        qc[h, 0:N, :] = jnp.where(low, right, 0.0).astype(BF16)
        qc[h, N : 2 * N, :] = jnp.where(low, 0.0, right).astype(BF16)
        cols = nt(xin[h], pt[h]).astype(BF16)
        xp[h] = cols
        rq[h, 0:E, :] = cols[128:192]
        rq[h, E:128, :] = zero
        rc[h, 0:E, :] = zero
        rc[h, E:128, :] = cols[192:256]

    def fill_bias(ref, at, rows, lanes, key_place, group):
        lq = level_of(lax.broadcasted_iota(jnp.int32, (rows, lanes), 1))
        mult = jnp.minimum(lq, level_of(key_place)) - (group - 1)
        value = jnp.where(mult > 0, jnp.log2(jnp.maximum(mult, 1).astype(F32)), NEG)
        ref[at : at + rows, :] = value

    wide = lax.broadcasted_iota(jnp.int32, (256, 256), 0)
    r256 = lax.broadcasted_iota(jnp.int32, (256, 128), 0)
    fill_bias(bias0, 0, 256, 256, wide, 0)

    def forward(score, values):
        peak = jnp.max(score, axis=0, keepdims=True)
        expo = jnp.exp2(score - peak)
        total = jnp.sum(expo, axis=0, keepdims=True)
        return peak, expo, total, nn(values, expo.astype(BF16))[E:128]

    local = [[] for _ in range(HEADS)]
    part1 = [None] * HEADS
    parts2 = [[] for _ in range(HEADS)]

    def local_forward(h, t):
        qs = slice(256 * t, 256 * t + 256)
        score = nn(own[:, head_lanes(h)], rq[h, :, qs]) * SCALE2
        if t == 0:
            score = jnp.concatenate([score[0:256] + bias0[...], score[256:512]], axis=0)
        peak, expo, total, mix = forward(score, xp[h, 0:128, :])
        e0[h, :, qs] = expo
        num[h, :, qs] = mix
        local[h].append((peak, total))

    eye = jnp.where(
        lax.broadcasted_iota(jnp.int32, (128, 128), 0)
        == lax.broadcasted_iota(jnp.int32, (128, 128), 1),
        1.0,
        0.0,
    ).astype(BF16)

    def remote_forward(h, a, b):
        ks = slice(256 + a, 256 + b)
        keys = rk[ks, head_lanes(h)]
        rkt[h, :, ks] = nt(eye, keys).astype(BF16)
        if a >= 256:
            dp2[h, a - 256 : b - 256, :] = nn(keys, rc[h, :, 0:128])
        score = nn(keys, rq[h, :, 0:128]) * SCALE2 + bias2[a:b, :]
        peak, expo, total, mix = forward(score, rkt[h, :, ks])
        e2[h, a:b, :] = expo
        at = 256 + 128 * len(parts2[h])
        nums[h, :, at : at + 128] = mix
        parts2[h].append((peak, total, at, a, b))

    local_forward(0, 0)

    need("z32", "z48")
    rk[S6 : S6 + 16, :] = jnp.concatenate(
        [t32[...].astype(F32)[0:8], t48[...].astype(F32)[8:16]], axis=0
    ).astype(BF16)
    for e in (1, 2, 3, 4, 8, 12):
        move(f"p{e}", e, rk, S6, rk, S6 + 16 * e, 16)
    for b in (1, 2):
        need(f"ya{b}")
        for e in (4, 8, 12):
            move(f"x{e}_{b}", e, rk, Y_AT[b], rk, slot_at(e + b), X_ROWS[e])
    for e in (4, 12, 8):
        need(f"x{e}_0")
        move(f"x{e}_3", 3, rk, slot_at(e), rk, slot_at(e + 3), X_ROWS[e])
    move("yb1", 1, own, 64, rk, Y_AT[1] + 64, 192)
    move("yb3", 3, own, 64, rk, Y_AT[3] + 64, 64)
    move("yb2", 2, own, 64, rk, Y_AT[2] + 64, 64)

    def last_z(*slots):
        for d in slots:
            src = Y_AT[d] if d < 4 else slot_at(d)
            move(f"zl{d}", 16, rk, src, rk, S5 + 16 * d, 16)

    need("ya3")
    last_z(1, 2, 3, 4, 8, 12)

    local_forward(1, 0)
    need("p1", "p2", "p3")
    for e in (4, 8, 12):
        move(f"pp{e}", e, rk, S6 + 16, rk, S6 + 16 * e + 16, 48)
    for e in (4, 12, 8):
        need(f"x{e}_1")
        last_z(e + 1)
    for e in (4, 12, 8):
        need(f"x{e}_2")
        last_z(e + 2)
    for e in (4, 12, 8):
        need(f"x{e}_3")
        last_z(e + 3)

    local_forward(2, 0)
    fill_bias(bias2, 256, 256, 128, r256 & 63, 3)
    fill_bias(bias2, 512, 256, 128, r256 & 31, 4)
    fill_bias(bias2, 768, 256, 128, r256 & 15, 5)
    fill_bias(bias2, 1024, 256, 128, r256 & 7, 6)
    for h in range(HEADS):
        remote_forward(h, 256, 768)
    fill_bias(bias1, 0, 256, 256, wide, 1)
    fill_bias(bias2, 0, 256, 128, r256 & 127, 2)
    need("yb1", "yb2", "yb3")
    for h in range(HEADS):
        keys = rk[0:256, head_lanes(h)]
        rkt[h, :, 0:256] = nt(eye, keys).astype(BF16)
        score = nn(keys, rq[h, :, 0:256]) * SCALE2 + bias1[...]
        peak, expo, total, mix = forward(score, rkt[h, :, 0:256])
        e1[h] = expo
        nums[h, :, 0:256] = mix
        part1[h] = (peak, total)
        remote_forward(h, 0, 256)
    for e in (4, 8, 12):
        need(f"p{e}", f"pp{e}")
    for h in range(HEADS):
        remote_forward(h, 1024, 1280)
    need(*(f"zl{d}" for d in range(16)))
    for h in range(HEADS):
        remote_forward(h, 768, 1024)

    def combine(h, lo, hi):
        t = lo // 256
        ls = slice(lo - 256 * t, hi - 256 * t)
        pieces = [(local[h][t][0][:, ls], local[h][t][1][:, ls], num[h, :, lo:hi])]
        if hi <= 256:
            pieces.append((part1[h][0][:, lo:hi], part1[h][1][:, lo:hi], nums[h, :, lo:hi]))
        if hi <= 128:
            for peak, total, at, _, _ in parts2[h]:
                pieces.append((peak, total, nums[h, :, at : at + 128]))
        top = pieces[0][0]
        for peak, _, _ in pieces[1:]:
            top = jnp.maximum(top, peak)
        factors = [jnp.exp2(peak - top) for peak, _, _ in pieces]
        inv = 1.0 / sum(f * total for f, (_, total, _) in zip(factors, pieces))
        gains = [f * inv for f in factors]
        attended = sum(g * mix for g, (_, _, mix) in zip(gains, pieces)).astype(BF16)
        cot = xp[h, 192:256, lo:hi].astype(F32)
        delta = jnp.sum(cot * attended.astype(F32), axis=0, keepdims=True)
        xp[h, 192:256, lo:hi] = attended
        return gains, delta

    def backward(h, dprob, expo, gain, delta, nq):
        probs = expo * gain
        dscore = (probs * (dprob - delta)).astype(BF16)
        both = jnp.concatenate([dscore, probs.astype(BF16)], axis=1)
        right = jnp.concatenate([qc[h, 0:nq, :], qc[h, N : N + nq, :]], axis=0)
        return dscore, nn(both, right)

    def remote_backward(h, which):
        _, _, _, a, b = parts2[h][which]
        gains, delta = first[h]
        if a >= 256:
            dprob = dp2[h, a - 256 : b - 256, :]
        else:
            dprob = nn(rk[256 + a : 256 + b, head_lanes(h)], rc[h, :, 0:128])
        dscore, dkv = backward(h, dprob, e2[h, a:b, :], gains[2 + which], delta, 128)
        return dkv, dscore, rkt[h, :, 256 + a : 256 + b]

    first = [combine(h, 0, 128) for h in range(HEADS)]
    z_at = {4: 0, 8: 64, 12: 128}
    queries = [[] for _ in range(HEADS)]
    for h in range(HEADS):
        hs = head_lanes(h)
        for which, at, kept in ((3, S5, 0), (2, S6, 64)):
            dkv, *rest = remote_backward(h, which)
            queries[h].append(rest)
            gsend[at : at + 256, hs] = dkv.astype(BF16)
            pacc[kept : kept + 64, hs] = dkv[0:64]
    for e in (4, 8, 12):
        move(f"gp5{e}", e, gsend, S5 + 16 * e, rz5, z_at[e], 64)
        move(f"gp6{e}", e, gsend, S6 + 16 * e, rz6, z_at[e], 64)
    r3_at = {4: 0, 8: 64, 12: 96}
    x12_at = {4: 0, 8: 128, 12: 192}
    for h in range(HEADS):
        hs = head_lanes(h)
        dkv, *rest = remote_backward(h, 0)
        queries[h].append(rest)
        gsend[512:1024, hs] = dkv.astype(BF16)
        xacc[0:64, hs] = dkv[0:64]
        xacc[64:96, hs] = dkv[256:288]
        xacc[96:128, hs] = dkv[384:416]
    for e in (4, 8, 12):
        move(f"g{e}_3", 3, gsend, slot_at(e + 3), r3, r3_at[e], X_ROWS[e])
    for e in (4, 8, 12):
        move(f"g{e}_12", e, gsend, slot_at(e + 1), rx12, x12_at[e], 2 * X_ROWS[e])

    second = [combine(h, 128, 256) for h in range(HEADS)]
    for h in range(HEADS):
        hs = head_lanes(h)
        delta = jnp.concatenate([first[h][1], second[h][1]], axis=1)
        gain = jnp.concatenate([first[h][0][1], second[h][0][1]], axis=1)
        dprob = nn(rk[0:256, hs], rc[h, :, 0:256])
        dscore, dkv = backward(h, dprob, e1[h], gain, delta, 256)
        dqa[h] = nn(rkt[h, :, 0:256], dscore)[0:E]
        yacc[0:64, hs] = dkv[0:64]
        gsend[64:256, hs] = dkv[64:256].astype(BF16)
        dkv, *rest = remote_backward(h, 1)
        dqa[h, :, 0:128] += sum(nn(values, ds)[0:E] for ds, values in [*queries[h], rest])
        yacc[64:128, hs] = dkv[0:64]
        gsend[320:512, hs] = dkv[64:256].astype(BF16)
    move("gy3", 3, gsend, 384, ry, 384, 128)
    move("gy1", 1, gsend, 64, ry, 64, 192)
    move("gy2", 2, gsend, 320, ry, 320, 64)

    x0_at = {4: 0, 8: 64, 12: 96}
    for e in (4, 8, 12):
        n, at = X_ROWS[e], x0_at[e]
        need(f"g{e}_3")
        total = xacc[at : at + n, :] + r3[at : at + n, :].astype(F32)
        gsend[slot_at(e) : slot_at(e) + n, :] = total.astype(BF16)
        move(f"g{e}_0", e, gsend, slot_at(e), rx0, at, n)

    def local_backward(h):
        local_forward(h, 1)
        ranges = (first[h], second[h], combine(h, 256, 512))
        gain = jnp.concatenate([gains[0] for gains, _ in ranges], axis=1)
        delta = jnp.concatenate([part for _, part in ranges], axis=1)
        dprob = nn(own[:, head_lanes(h)], rc[h])
        dscore, dkv = backward(h, dprob, e0[h], gain, delta, N)
        oacc[:, head_lanes(h)] = dkv
        dq = nn(xp[h, 0:128, :], dscore)[0:E]
        dq = jnp.concatenate([dq[:, 0:256] + dqa[h], dq[:, 256:512]], axis=1)
        done = nn(jnp.concatenate([xp[h, 192:256, :], dq.astype(BF16)], axis=0), pt[h])
        out[0, h] = done[0:E].astype(BF16)
        out[1, h] = (done[E:128] * 0.125).astype(BF16)

    local_backward(0)

    for e in (4, 8, 12):
        need(f"gp5{e}", f"gp6{e}")
    for b in (1, 2, 3):
        bs = slice(16 * b, 16 * b + 16)
        for part, got in ((0, rz5), (1, rz6)):
            total = pacc[64 * part + 16 * b : 64 * part + 16 * b + 16, :]
            for e in (4, 8, 12):
                total = total + got[z_at[e] + 16 * b : z_at[e] + 16 * b + 16, :].astype(F32)
            at = 32 * (b - 1) + 16 * part
            pz[at : at + 16, :] = total.astype(BF16)
        move(f"gpy{b}", b, pz, 32 * (b - 1), ryz, 32 * (b - 1), 32)
    for e in (4, 8, 12):
        need(f"g{e}_12")
    for b in (1, 2):
        part = yacc[64 * (b - 1) : 64 * b, :] + rx12[64 * (b - 1) : 64 * b, :].astype(F32)
        small = rx12[96 + 32 * b : 128 + 32 * b, :].astype(F32) + rx12[
            160 + 32 * b : 192 + 32 * b, :
        ].astype(F32)
        gsend[Y_AT[b] : Y_AT[b] + 32, :] = (part[0:32] + small).astype(BF16)
        gsend[Y_AT[b] + 32 : Y_AT[b] + 64, :] = part[32:64].astype(BF16)
        move(f"gya{b}", b, gsend, Y_AT[b], ry, Y_AT[b], 64)

    local_backward(1)

    need("gpy1", "gpy2", "gpy3")
    for part, got in ((0, rz5), (1, rz6)):
        total = pacc[64 * part : 64 * part + 16, :]
        for e in (4, 8, 12):
            total = total + got[z_at[e] : z_at[e] + 16, :].astype(F32)
        for b in (0, 1, 2):
            total = total + ryz[32 * b + 16 * part : 32 * b + 16 * part + 16, :].astype(F32)
        gsend[S5 + 256 * part : S5 + 256 * part + 16, :] = total.astype(BF16)
    move("gz16", 16, gsend, S5, rzz, 0, 16)
    move("gz32", 32, gsend, S6, rzz, 16, 16)
    move("gz48", 48, gsend, S6, rzz, 32, 16)

    local_backward(2)

    need("gy1", "gy2", "gy3")
    for h in range(HEADS):
        hs = head_lanes(h)
        b256 = oacc[128:256, hs] + ry[128:256, hs].astype(F32)
        whole = jnp.concatenate([b256, oacc[256:512, hs]], axis=0)
        early[h] = nn(whole.T.astype(BF16), pt[h, 128:512, :])
        b128 = oacc[64:128, hs]
        for b in (1, 2, 3):
            b128 = b128 + ry[Y_AT[b] + 64 : Y_AT[b] + 128, hs].astype(F32)
        oacc[64:128, hs] = b128

    need("g4_0", "g8_0", "g12_0", "gya1", "gya2", "gz16", "gz32", "gz48")
    for h in range(HEADS):
        hs = head_lanes(h)
        a = oacc[0:64, hs] + rx0[0:64, hs].astype(F32)
        for b in (1, 2, 3):
            a = a + ry[Y_AT[b] : Y_AT[b] + 64, hs].astype(F32)
        a32 = a[0:32] + rx0[64:96, hs].astype(F32) + rx0[96:128, hs].astype(F32)
        a16 = a32[0:16] + rzz[0:16, hs].astype(F32)
        a8 = a16[0:8] + rzz[16:32, hs].astype(F32)[0:8] + rzz[32:48, hs].astype(F32)[8:16]
        whole = jnp.concatenate([a8, a16[8:16], a32[16:32], a[32:64], oacc[64:128, hs]], axis=0)
        done = early[h] + nn(whole.T.astype(BF16), pt[h, 0:128, :])
        out[2, h] = (done[0:E] * 0.125).astype(BF16)
        out[3, h] = done[E:128].astype(BF16)
    for copy in copies.values():
        copy.wait_send()


def hand_out(res, o_hbm, gq_hbm, gk_hbm, gv_hbm, sem):
    stores = [
        pltpu.make_async_copy(res.at[at], dst, sem.at[at])
        for at, dst in enumerate((o_hbm, gq_hbm, gk_hbm, gv_hbm))
    ]
    for store in stores:
        store.start()
    for store in stores:
        store.wait()


COPIES = 72


def per_device(tile_query, tile_key, tile_value, out_cotangent):
    shape = (HEADS, E, N)
    args = [
        pltpu.with_memory_space_constraint(a.reshape(shape), pltpu.HBM)
        for a in (tile_query, tile_key, tile_value, out_cotangent)
    ]
    vm = pltpu.VMEM
    anywhere = pl.BlockSpec(memory_space=pl.ANY)
    res = pl.pallas_call(
        body,
        out_shape=jax.ShapeDtypeStruct((4, *shape), BF16),
        in_specs=[anywhere] * 4,
        out_specs=pl.BlockSpec(memory_space=pltpu.VMEM),
        scratch_shapes=[
            vm((HEADS, 256, N), BF16),
            vm((HEADS, N, N), BF16),
            vm((N, W), BF16),
            vm((16, W), BF16),
            vm((HEADS, 2 * N, 128), BF16),
            vm((HEADS, 256, N), BF16),
            vm((HEADS, 128, N), BF16),
            vm((HEADS, 128, N), BF16),
            vm((256, 256), F32),
            vm((256, 256), F32),
            vm((1280, 128), F32),
            vm((HEADS, N, N), F32),
            vm((HEADS, 256, 256), F32),
            vm((HEADS, 1280, 128), F32),
            vm((HEADS, 1024, 128), F32),
            vm((HEADS, E, N), F32),
            vm((HEADS, E, 768), F32),
            vm((HEADS, E, 256), F32),
            vm((HEADS, 128, N), F32),
            vm((ROWS, W), BF16),
            vm((HEADS, 128, ROWS), BF16),
            vm((16, W), BF16),
            vm((16, W), BF16),
            vm((ROWS, W), BF16),
            vm((128, W), F32),
            vm((128, W), F32),
            vm((128, W), F32),
            vm((N, W), F32),
            vm((128, W), BF16),
            vm((256, W), BF16),
            vm((128, W), BF16),
            vm((192, W), BF16),
            vm((192, W), BF16),
            vm((512, W), BF16),
            vm((96, W), BF16),
            vm((96, W), BF16),
            vm((48, W), BF16),
            pltpu.SemaphoreType.DMA((4,)),
            pltpu.SemaphoreType.DMA((COPIES,)),
            pltpu.SemaphoreType.DMA((COPIES,)),
        ],
        compiler_params=pltpu.CompilerParams(
            collective_id=0, has_side_effects=True, vmem_limit_bytes=44 * 2**20
        ),
        name="dilated",
    )(*args)
    outs = pl.pallas_call(
        hand_out,
        out_shape=[jax.ShapeDtypeStruct((HEADS * E, N), BF16)] * 4,
        in_specs=[anywhere],
        out_specs=[anywhere] * 4,
        scratch_shapes=[
            pltpu.SemaphoreType.DMA((4,)),
        ],
        compiler_params=pltpu.CompilerParams(vmem_limit_bytes=2**20),
        name="outputs",
    )(res.reshape(4, HEADS * E, N))
    return tuple(outs)


def solution(mesh):
    spec = P("head", "seq")
    return jax.shard_map(
        per_device, mesh=mesh, in_specs=(spec,) * 4, out_specs=(spec,) * 4, check_vma=False
    )
```

```python
import math

import jax
import jax.numpy as jnp
from jax import lax
from jax.experimental import pallas as pl
from jax.experimental.pallas import tpu as pltpu
from jax.sharding import PartitionSpec as P

E = 64
HEADS = 3
N = 512
W = HEADS * 128
F32 = jnp.float32
BF16 = jnp.bfloat16
NEG = -1e30
SCALE2 = math.log2(math.e) / math.sqrt(E)

ROWS = 1536
Y_AT, Y_ROWS = {1: 0, 2: 256, 3: 384}, {1: 256, 2: 128, 3: 128}
X_AT, X_ROWS = {4: 512, 8: 768, 12: 896}, {4: 64, 8: 32, 12: 32}
S5, S6 = 1024, 1280


def slot_at(d):
    return X_AT[d // 4 * 4] + X_ROWS[d // 4 * 4] * (d % 4)


def nn(a, b):
    return lax.dot_general(a, b, (((1,), (0,)), ((), ())), preferred_element_type=F32)


def nt(a, b):
    return lax.dot_general(a, b, (((1,), (1,)), ((), ())), preferred_element_type=F32)


def level_of(index):
    level = jnp.zeros(index.shape, jnp.int32)
    for bound in (8, 16, 32, 64, 128, 256):
        level = level + (index < bound).astype(jnp.int32)
    return level


def body(
    q_hbm, k_hbm, v_hbm, c_hbm, out,
    xin, pt, own, d6, qc, xp, rq, rc, bias0, bias1, bias2,
    e0, e1, e2, dp2, num, nums, dqa, early,
    rk, rkt, t32, t48, gsend, yacc, xacc, pacc, oacc,
    rx0, rx12, r3, rz5, rz6, ry, pz, ryz, rzz,
    in_sem, send_sem, recv_sem,
):
    me = lax.axis_index("seq")
    head0 = lax.axis_index("head") * HEADS
    z, x, y = lax.div(me, 16), lax.rem(lax.div(me, 4), 4), lax.rem(me, 4)

    def flipped(v, bits):
        if bits == 0:
            return v
        if bits == 1:
            return v + 1 - 2 * lax.rem(v, 2)
        if bits == 2:
            return lax.rem(v + 2, 4)
        return 3 - v

    peer = {e: flipped(z, e // 16) * 16 + flipped(x, e // 4 % 4) * 4 + flipped(y, e % 4)
            for e in (1, 2, 3, 4, 8, 12, 16, 32, 48)}

    loads = []
    for at, src in enumerate((k_hbm, v_hbm, q_hbm, c_hbm)):
        load = pltpu.make_async_copy(src, xin.at[:, pl.ds(64 * at, 64), :], in_sem.at[at])
        load.start()
        loads.append(load)
    barrier = pltpu.get_barrier_semaphore()
    for e in peer:
        pl.semaphore_signal(
            barrier, inc=1, device_id={"seq": peer[e]}, device_id_type=pl.DeviceIdType.MESH
        )

    copies, landed = {}, set()

    def send(key, src, dst, e):
        at = len(copies)
        copies[key] = pltpu.make_async_remote_copy(
            src_ref=src,
            dst_ref=dst,
            send_sem=send_sem.at[at],
            recv_sem=recv_sem.at[at],
            device_id={"seq": peer[e]},
            device_id_type=pl.DeviceIdType.MESH,
        )
        copies[key].start()

    def need(*keys):
        for key in keys:
            if key not in landed:
                copies[key].wait_recv()
                landed.add(key)

    def move(key, e, src, a, dst, b, n):
        send(key, src.at[a : a + n], dst.at[b : b + n], e)

    def head_lanes(h):
        return slice(128 * h, 128 * h + 128)

    def one_hot(lo, hi):
        place = lax.broadcasted_iota(jnp.int32, (hi - lo, 128), 0) + lo
        lane = lax.broadcasted_iota(jnp.int32, (8, 128), 1)
        u = 64 * place
        for bits in range(4, hi.bit_length()):
            u = jnp.where(place >= 1 << (bits - 1), ((2 * place + 1) << (9 - bits)) & (N - 1), u)
        for h in range(HEADS):
            for t in range(4):
                tile = (lane + (128 * t + N) - (head0 + h)) & (N - 1)
                hot = u == jnp.broadcast_to(tile[0:1], (hi - lo, 128))
                pt[h, lo:hi, 128 * t : 128 * t + 128] = jnp.where(hot, 1.0, 0.0).astype(BF16)

    one_hot(0, 64)
    for load in loads[0:2]:
        load.wait()
    for h in range(HEADS):
        rows = nt(pt[h, 0:64, :], xin[h, 0:128, :])
        own[0:64, head_lanes(h)] = rows.astype(BF16)
        d6[:, head_lanes(h)] = jnp.concatenate([rows[0:8]] * 2, axis=0).astype(BF16)

    pl.semaphore_wait(barrier, len(peer))
    move("x4_0", 4, own, 0, rk, slot_at(4), 64)
    move("ya1", 1, own, 0, rk, Y_AT[1], 64)
    send("z32", d6, t32, 32)
    send("z48", d6, t48, 48)
    move("ya3", 3, own, 0, rk, Y_AT[3], 64)
    move("x8_0", 8, own, 0, rk, slot_at(8), 32)
    move("ya2", 2, own, 0, rk, Y_AT[2], 64)
    move("x12_0", 12, own, 0, rk, slot_at(12), 32)
    move("zl0", 16, own, 0, rk, S5, 16)

    one_hot(64, N)
    for load in loads[2:4]:
        load.wait()
    low = lax.broadcasted_iota(jnp.int32, (N, 128), 1) < E
    zero = jnp.zeros((E, N), BF16)
    for h in range(HEADS):
        own[64:N, head_lanes(h)] = nt(pt[h, 64:N, :], xin[h, 0:128, :]).astype(BF16)
        right = nt(pt[h], xin[h, 128:256, :])
        qc[h, 0:N, :] = jnp.where(low, right, 0.0).astype(BF16)
        qc[h, N : 2 * N, :] = jnp.where(low, 0.0, right).astype(BF16)
        cols = nt(xin[h], pt[h]).astype(BF16)
        xp[h] = cols
        rq[h, 0:E, :] = cols[128:192]
        rq[h, E:128, :] = zero
        rc[h, 0:E, :] = zero
        rc[h, E:128, :] = cols[192:256]

    def fill_bias(ref, at, rows, lanes, key_place, group):
        lq = level_of(lax.broadcasted_iota(jnp.int32, (rows, lanes), 1))
        mult = jnp.minimum(lq, level_of(key_place)) - (group - 1)
        value = jnp.where(mult > 0, jnp.log2(jnp.maximum(mult, 1).astype(F32)), NEG)
        ref[at : at + rows, :] = value

    wide = lax.broadcasted_iota(jnp.int32, (256, 256), 0)
    r256 = lax.broadcasted_iota(jnp.int32, (256, 128), 0)
    fill_bias(bias0, 0, 256, 256, wide, 0)

    def forward(score, values):
        peak = jnp.max(score, axis=0, keepdims=True)
        expo = jnp.exp2(score - peak)
        total = jnp.sum(expo, axis=0, keepdims=True)
        return peak, expo, total, nn(values, expo.astype(BF16))[E:128]

    local = [[] for _ in range(HEADS)]
    part1 = [None] * HEADS
    parts2 = [[] for _ in range(HEADS)]

    def local_forward(h, t):
        qs = slice(256 * t, 256 * t + 256)
        score = nn(own[:, head_lanes(h)], rq[h, :, qs]) * SCALE2
        if t == 0:
            score = jnp.concatenate([score[0:256] + bias0[...], score[256:512]], axis=0)
        peak, expo, total, mix = forward(score, xp[h, 0:128, :])
        e0[h, :, qs] = expo
        num[h, :, qs] = mix
        local[h].append((peak, total))

    eye = jnp.where(
        lax.broadcasted_iota(jnp.int32, (128, 128), 0)
        == lax.broadcasted_iota(jnp.int32, (128, 128), 1),
        1.0,
        0.0,
    ).astype(BF16)

    def remote_forward(h, a, b):
        ks = slice(256 + a, 256 + b)
        keys = rk[ks, head_lanes(h)]
        rkt[h, :, ks] = nt(eye, keys).astype(BF16)
        if a >= 256:
            dp2[h, a - 256 : b - 256, :] = nn(keys, rc[h, :, 0:128])
        score = nn(keys, rq[h, :, 0:128]) * SCALE2 + bias2[a:b, :]
        peak, expo, total, mix = forward(score, rkt[h, :, ks])
        e2[h, a:b, :] = expo
        at = 256 + 128 * len(parts2[h])
        nums[h, :, at : at + 128] = mix
        parts2[h].append((peak, total, at, a, b))

    local_forward(0, 0)

    need("z32", "z48")
    rk[S6 : S6 + 16, :] = jnp.concatenate(
        [t32[...].astype(F32)[0:8], t48[...].astype(F32)[8:16]], axis=0
    ).astype(BF16)
    for e in (1, 2, 3, 4, 8, 12):
        move(f"p{e}", e, rk, S6, rk, S6 + 16 * e, 16)
    for b in (1, 2):
        need(f"ya{b}")
        for e in (4, 8, 12):
            move(f"x{e}_{b}", e, rk, Y_AT[b], rk, slot_at(e + b), X_ROWS[e])
    for e in (4, 12, 8):
        need(f"x{e}_0")
        move(f"x{e}_3", 3, rk, slot_at(e), rk, slot_at(e + 3), X_ROWS[e])
    move("yb1", 1, own, 64, rk, Y_AT[1] + 64, 192)
    move("yb3", 3, own, 64, rk, Y_AT[3] + 64, 64)
    move("yb2", 2, own, 64, rk, Y_AT[2] + 64, 64)

    def last_z(*slots):
        for d in slots:
            src = Y_AT[d] if d < 4 else slot_at(d)
            move(f"zl{d}", 16, rk, src, rk, S5 + 16 * d, 16)

    need("ya3")
    last_z(1, 2, 3, 4, 8, 12)

    local_forward(1, 0)
    need("p1", "p2", "p3")
    for e in (4, 8, 12):
        move(f"pp{e}", e, rk, S6 + 16, rk, S6 + 16 * e + 16, 48)
    for e in (4, 12, 8):
        need(f"x{e}_1")
        last_z(e + 1)
    for e in (4, 12, 8):
        need(f"x{e}_2")
        last_z(e + 2)
    for e in (4, 12, 8):
        need(f"x{e}_3")
        last_z(e + 3)

    local_forward(2, 0)
    fill_bias(bias2, 256, 256, 128, r256 & 63, 3)
    fill_bias(bias2, 512, 256, 128, r256 & 31, 4)
    fill_bias(bias2, 768, 256, 128, r256 & 15, 5)
    fill_bias(bias2, 1024, 256, 128, r256 & 7, 6)
    for h in range(HEADS):
        remote_forward(h, 256, 768)
    fill_bias(bias1, 0, 256, 256, wide, 1)
    fill_bias(bias2, 0, 256, 128, r256 & 127, 2)
    need("yb1", "yb2", "yb3")
    for h in range(HEADS):
        keys = rk[0:256, head_lanes(h)]
        rkt[h, :, 0:256] = nt(eye, keys).astype(BF16)
        score = nn(keys, rq[h, :, 0:256]) * SCALE2 + bias1[...]
        peak, expo, total, mix = forward(score, rkt[h, :, 0:256])
        e1[h] = expo
        nums[h, :, 0:256] = mix
        part1[h] = (peak, total)
        remote_forward(h, 0, 256)
    for e in (4, 8, 12):
        need(f"p{e}", f"pp{e}")
    for h in range(HEADS):
        remote_forward(h, 1024, 1280)
    need(*(f"zl{d}" for d in range(16)))
    for h in range(HEADS):
        remote_forward(h, 768, 1024)

    def combine(h, lo, hi):
        t = lo // 256
        ls = slice(lo - 256 * t, hi - 256 * t)
        pieces = [(local[h][t][0][:, ls], local[h][t][1][:, ls], num[h, :, lo:hi])]
        if hi <= 256:
            pieces.append((part1[h][0][:, lo:hi], part1[h][1][:, lo:hi], nums[h, :, lo:hi]))
        if hi <= 128:
            for peak, total, at, _, _ in parts2[h]:
                pieces.append((peak, total, nums[h, :, at : at + 128]))
        top = pieces[0][0]
        for peak, _, _ in pieces[1:]:
            top = jnp.maximum(top, peak)
        factors = [jnp.exp2(peak - top) for peak, _, _ in pieces]
        inv = 1.0 / sum(f * total for f, (_, total, _) in zip(factors, pieces))
        gains = [f * inv for f in factors]
        attended = sum(g * mix for g, (_, _, mix) in zip(gains, pieces)).astype(BF16)
        cot = xp[h, 192:256, lo:hi].astype(F32)
        delta = jnp.sum(cot * attended.astype(F32), axis=0, keepdims=True)
        xp[h, 192:256, lo:hi] = attended
        return gains, delta

    def backward(h, dprob, expo, gain, delta, nq):
        probs = expo * gain
        dscore = (probs * (dprob - delta)).astype(BF16)
        both = jnp.concatenate([dscore, probs.astype(BF16)], axis=1)
        right = jnp.concatenate([qc[h, 0:nq, :], qc[h, N : N + nq, :]], axis=0)
        return dscore, nn(both, right)

    def remote_backward(h, which):
        _, _, _, a, b = parts2[h][which]
        gains, delta = first[h]
        if a >= 256:
            dprob = dp2[h, a - 256 : b - 256, :]
        else:
            dprob = nn(rk[256 + a : 256 + b, head_lanes(h)], rc[h, :, 0:128])
        dscore, dkv = backward(h, dprob, e2[h, a:b, :], gains[2 + which], delta, 128)
        return dkv, dscore, rkt[h, :, 256 + a : 256 + b]

    first = [combine(h, 0, 128) for h in range(HEADS)]
    z_at = {4: 0, 8: 64, 12: 128}
    queries = [[] for _ in range(HEADS)]
    for h in range(HEADS):
        hs = head_lanes(h)
        for which, at, kept in ((3, S5, 0), (2, S6, 64)):
            dkv, *rest = remote_backward(h, which)
            queries[h].append(rest)
            gsend[at : at + 256, hs] = dkv.astype(BF16)
            pacc[kept : kept + 64, hs] = dkv[0:64]
    for e in (8, 4, 12):
        move(f"gp5{e}", e, gsend, S5 + 16 * e, rz5, z_at[e], 64)
        move(f"gp6{e}", e, gsend, S6 + 16 * e, rz6, z_at[e], 64)
    r3_at = {4: 0, 8: 64, 12: 96}
    x12_at = {4: 0, 8: 128, 12: 192}
    for h in range(HEADS):
        hs = head_lanes(h)
        dkv, *rest = remote_backward(h, 0)
        queries[h].append(rest)
        gsend[512:1024, hs] = dkv.astype(BF16)
        xacc[0:64, hs] = dkv[0:64]
        xacc[64:96, hs] = dkv[256:288]
        xacc[96:128, hs] = dkv[384:416]
    for e in (4, 8, 12):
        move(f"g{e}_3", 3, gsend, slot_at(e + 3), r3, r3_at[e], X_ROWS[e])
    for e in (4, 8, 12):
        move(f"g{e}_12", e, gsend, slot_at(e + 1), rx12, x12_at[e], 2 * X_ROWS[e])

    second = [combine(h, 128, 256) for h in range(HEADS)]
    for h in range(HEADS):
        hs = head_lanes(h)
        delta = jnp.concatenate([first[h][1], second[h][1]], axis=1)
        gain = jnp.concatenate([first[h][0][1], second[h][0][1]], axis=1)
        dprob = nn(rk[0:256, hs], rc[h, :, 0:256])
        dscore, dkv = backward(h, dprob, e1[h], gain, delta, 256)
        dqa[h] = nn(rkt[h, :, 0:256], dscore)[0:E]
        yacc[0:64, hs] = dkv[0:64]
        gsend[64:256, hs] = dkv[64:256].astype(BF16)
        dkv, *rest = remote_backward(h, 1)
        dqa[h, :, 0:128] += sum(nn(values, ds)[0:E] for ds, values in [*queries[h], rest])
        yacc[64:128, hs] = dkv[0:64]
        gsend[320:512, hs] = dkv[64:256].astype(BF16)
    move("gy3", 3, gsend, 384, ry, 384, 128)
    move("gy1", 1, gsend, 64, ry, 64, 192)
    move("gy2", 2, gsend, 320, ry, 320, 64)

    x0_at = {4: 0, 8: 64, 12: 96}
    for e in (4, 8, 12):
        n, at = X_ROWS[e], x0_at[e]
        need(f"g{e}_3")
        total = xacc[at : at + n, :] + r3[at : at + n, :].astype(F32)
        gsend[slot_at(e) : slot_at(e) + n, :] = total.astype(BF16)
        move(f"g{e}_0", e, gsend, slot_at(e), rx0, at, n)

    def local_backward(h):
        local_forward(h, 1)
        ranges = (first[h], second[h], combine(h, 256, 512))
        gain = jnp.concatenate([gains[0] for gains, _ in ranges], axis=1)
        delta = jnp.concatenate([part for _, part in ranges], axis=1)
        dprob = nn(own[:, head_lanes(h)], rc[h])
        dscore, dkv = backward(h, dprob, e0[h], gain, delta, N)
        oacc[:, head_lanes(h)] = dkv
        dq = nn(xp[h, 0:128, :], dscore)[0:E]
        dq = jnp.concatenate([dq[:, 0:256] + dqa[h], dq[:, 256:512]], axis=1)
        done = nn(jnp.concatenate([xp[h, 192:256, :], dq.astype(BF16)], axis=0), pt[h])
        out[0, h] = done[0:E].astype(BF16)
        out[1, h] = (done[E:128] * 0.125).astype(BF16)

    local_backward(0)

    for e in (4, 8, 12):
        need(f"gp5{e}", f"gp6{e}")
    for b in (1, 2, 3):
        bs = slice(16 * b, 16 * b + 16)
        for part, got in ((0, rz5), (1, rz6)):
            total = pacc[64 * part + 16 * b : 64 * part + 16 * b + 16, :]
            for e in (4, 8, 12):
                total = total + got[z_at[e] + 16 * b : z_at[e] + 16 * b + 16, :].astype(F32)
            at = 32 * (b - 1) + 16 * part
            pz[at : at + 16, :] = total.astype(BF16)
        move(f"gpy{b}", b, pz, 32 * (b - 1), ryz, 32 * (b - 1), 32)
    for e in (4, 8, 12):
        need(f"g{e}_12")
    for b in (1, 2):
        part = yacc[64 * (b - 1) : 64 * b, :] + rx12[64 * (b - 1) : 64 * b, :].astype(F32)
        small = rx12[96 + 32 * b : 128 + 32 * b, :].astype(F32) + rx12[
            160 + 32 * b : 192 + 32 * b, :
        ].astype(F32)
        gsend[Y_AT[b] : Y_AT[b] + 32, :] = (part[0:32] + small).astype(BF16)
        gsend[Y_AT[b] + 32 : Y_AT[b] + 64, :] = part[32:64].astype(BF16)
        move(f"gya{b}", b, gsend, Y_AT[b], ry, Y_AT[b], 64)

    local_backward(1)

    need("gpy1", "gpy2", "gpy3")
    for part, got in ((0, rz5), (1, rz6)):
        total = pacc[64 * part : 64 * part + 16, :]
        for e in (4, 8, 12):
            total = total + got[z_at[e] : z_at[e] + 16, :].astype(F32)
        for b in (0, 1, 2):
            total = total + ryz[32 * b + 16 * part : 32 * b + 16 * part + 16, :].astype(F32)
        gsend[S5 + 256 * part : S5 + 256 * part + 16, :] = total.astype(BF16)
    move("gz16", 16, gsend, S5, rzz, 0, 16)
    move("gz32", 32, gsend, S6, rzz, 16, 16)
    move("gz48", 48, gsend, S6, rzz, 32, 16)

    local_backward(2)

    need("gy1", "gy2", "gy3")
    for h in range(HEADS):
        hs = head_lanes(h)
        b256 = oacc[128:256, hs] + ry[128:256, hs].astype(F32)
        whole = jnp.concatenate([b256, oacc[256:512, hs]], axis=0)
        early[h] = nn(whole.T.astype(BF16), pt[h, 128:512, :])
        b128 = oacc[64:128, hs]
        for b in (1, 2, 3):
            b128 = b128 + ry[Y_AT[b] + 64 : Y_AT[b] + 128, hs].astype(F32)
        oacc[64:128, hs] = b128

    need("g4_0", "g8_0", "g12_0", "gya1", "gya2", "gz16", "gz32", "gz48")
    for h in range(HEADS):
        hs = head_lanes(h)
        a = oacc[0:64, hs] + rx0[0:64, hs].astype(F32)
        for b in (1, 2, 3):
            a = a + ry[Y_AT[b] : Y_AT[b] + 64, hs].astype(F32)
        a32 = a[0:32] + rx0[64:96, hs].astype(F32) + rx0[96:128, hs].astype(F32)
        a16 = a32[0:16] + rzz[0:16, hs].astype(F32)
        a8 = a16[0:8] + rzz[16:32, hs].astype(F32)[0:8] + rzz[32:48, hs].astype(F32)[8:16]
        whole = jnp.concatenate([a8, a16[8:16], a32[16:32], a[32:64], oacc[64:128, hs]], axis=0)
        done = early[h] + nn(whole.T.astype(BF16), pt[h, 0:128, :])
        out[2, h] = (done[0:E] * 0.125).astype(BF16)
        out[3, h] = done[E:128].astype(BF16)
    for copy in copies.values():
        copy.wait_send()


def hand_out(res, o_hbm, gq_hbm, gk_hbm, gv_hbm, sem):
    stores = [
        pltpu.make_async_copy(res.at[at], dst, sem.at[at])
        for at, dst in enumerate((o_hbm, gq_hbm, gk_hbm, gv_hbm))
    ]
    for store in stores:
        store.start()
    for store in stores:
        store.wait()


COPIES = 72


def per_device(tile_query, tile_key, tile_value, out_cotangent):
    shape = (HEADS, E, N)
    args = [
        pltpu.with_memory_space_constraint(a.reshape(shape), pltpu.HBM)
        for a in (tile_query, tile_key, tile_value, out_cotangent)
    ]
    vm = pltpu.VMEM
    anywhere = pl.BlockSpec(memory_space=pl.ANY)
    res = pl.pallas_call(
        body,
        out_shape=jax.ShapeDtypeStruct((4, *shape), BF16),
        in_specs=[anywhere] * 4,
        out_specs=pl.BlockSpec(memory_space=pltpu.VMEM),
        scratch_shapes=[
            vm((HEADS, 256, N), BF16),
            vm((HEADS, N, N), BF16),
            vm((N, W), BF16),
            vm((16, W), BF16),
            vm((HEADS, 2 * N, 128), BF16),
            vm((HEADS, 256, N), BF16),
            vm((HEADS, 128, N), BF16),
            vm((HEADS, 128, N), BF16),
            vm((256, 256), F32),
            vm((256, 256), F32),
            vm((1280, 128), F32),
            vm((HEADS, N, N), F32),
            vm((HEADS, 256, 256), F32),
            vm((HEADS, 1280, 128), F32),
            vm((HEADS, 1024, 128), F32),
            vm((HEADS, E, N), F32),
            vm((HEADS, E, 768), F32),
            vm((HEADS, E, 256), F32),
            vm((HEADS, 128, N), F32),
            vm((ROWS, W), BF16),
            vm((HEADS, 128, ROWS), BF16),
            vm((16, W), BF16),
            vm((16, W), BF16),
            vm((ROWS, W), BF16),
            vm((128, W), F32),
            vm((128, W), F32),
            vm((128, W), F32),
            vm((N, W), F32),
            vm((128, W), BF16),
            vm((256, W), BF16),
            vm((128, W), BF16),
            vm((192, W), BF16),
            vm((192, W), BF16),
            vm((512, W), BF16),
            vm((96, W), BF16),
            vm((96, W), BF16),
            vm((48, W), BF16),
            pltpu.SemaphoreType.DMA((4,)),
            pltpu.SemaphoreType.DMA((COPIES,)),
            pltpu.SemaphoreType.DMA((COPIES,)),
        ],
        compiler_params=pltpu.CompilerParams(
            collective_id=0, has_side_effects=True, vmem_limit_bytes=44 * 2**20
        ),
        name="dilated",
    )(*args)
    outs = pl.pallas_call(
        hand_out,
        out_shape=[jax.ShapeDtypeStruct((HEADS * E, N), BF16)] * 4,
        in_specs=[anywhere],
        out_specs=[anywhere] * 4,
        scratch_shapes=[
            pltpu.SemaphoreType.DMA((4,)),
        ],
        compiler_params=pltpu.CompilerParams(vmem_limit_bytes=2**20),
        name="outputs",
    )(res.reshape(4, HEADS * E, N))
    return tuple(outs)


def solution(mesh):
    spec = P("head", "seq")
    return jax.shard_map(
        per_device, mesh=mesh, in_specs=(spec,) * 4, out_specs=(spec,) * 4, check_vma=False
    )
```
